128 devices in a mesh: dp: 8 (over y, core), sp: 16 (over z, x).
Axes of the slice: x: 4, y: 4, z: 4, core: 2. Of those that a mesh axis runs over, the one named last changes fastest.
Arguments:
- queries: bfloat16 [8, 4096, 2048], P('dp', 'sp'), may hold values from -28 to 28
- keys: bfloat16 [8, 4096, 1024], P('dp', 'sp'), may hold values from -8 to 8
- values: bfloat16 [8, 4096, 1024], P('dp', 'sp'), may hold values from -6 to 6
- key_blocks: int32 [8, 16, 32, 8], P('dp', 'sp'), may hold values from 0 to 31, as said below
- block_counts: int32 [8, 16, 32], P('dp', 'sp'), may hold values from 1 to 8, as said below
- doc_lengths: int32 [8, 16], P('dp'), may hold values from 1 to 1024, 4096 in all within a row
- out_weight: bfloat16 [2048, 3072], P('sp'), may hold values from -0.125 to 0.125
- d_out: bfloat16 [8, 4096, 3072], P('dp', 'sp'), may hold values from -6 to 6
Outputs:
- layer_out: bfloat16 [8, 4096, 3072], P('dp', 'sp')
- grad_queries: bfloat16 [8, 4096, 2048], P('dp', 'sp')
- grad_keys: bfloat16 [8, 4096, 1024], P('dp', 'sp')
- grad_values: bfloat16 [8, 4096, 1024], P('dp', 'sp')
- grad_weight: float32 [2048, 3072], P('sp')
The draws below stay inside these ranges and needn't reach their ends.
Inputs may be any that keep to these rules, and one draw needn't show every extreme that they name: `key_blocks`: entry 0 of the list of query block b names b; the first block_counts entries name distinct blocks, none after b; later entries name other blocks. `block_counts`: for query block b at most b + 1.
All inputs are finite; a program needn't handle non-finite values.
Results may differ from the reference program's by a relative error of at most 0.022.
Values may be sent and summed in bfloat16 or wider, within the bound.
A program may use at most 128 MiB of HBM per device.

```python
import math
import jax
import jax.numpy as jnp
import numpy as np
from jax import lax

D = 3072
HEAD_SIZE = 128
KEY_VALUE_HEADS = 8
TOK_DEV = 256
MAXK = 8
NDOC = 16
QUERY_HEADS = 16
QW = 2048
SEQUENCE_LENGTH = 4096
SEQUENCE_COUNT = 8
NQB = 32
N_SP = 16


def block_plan(key):
    key_level, key_raw, key_head, key_score = jax.random.split(key, 4)
    level = jax.random.randint(key_level, (SEQUENCE_COUNT, QUERY_HEADS, 1), 1, MAXK)
    raw = jax.random.randint(key_raw, (SEQUENCE_COUNT, QUERY_HEADS, NQB), 0, 2 * MAXK)
    rows = jnp.arange(NQB, dtype=jnp.int32)
    counts = 1 + raw % (2 * level)
    counts = jnp.minimum(jnp.minimum(counts, MAXK), rows[None, None, :] + 1)
    forced = jax.random.randint(key_head, (SEQUENCE_COUNT, 1, 1), 0, QUERY_HEADS)
    heads = jnp.arange(QUERY_HEADS, dtype=jnp.int32)[None, :, None]
    counts = jnp.where((heads == forced) & (rows[None, None, :] == NQB - 1), MAXK, counts)
    scores = jax.random.randint(key_score, (SEQUENCE_COUNT, QUERY_HEADS, NQB, NQB), 1, 2 ** 20)
    query_rows = rows[:, None]
    key_cols = rows[None, :]
    scores = jnp.where(key_cols == query_rows, 2 ** 21, jnp.where(key_cols < query_rows, scores, 0))
    scores = scores * NQB + key_cols
    _, picked = lax.top_k(scores, MAXK)
    return (picked.astype(jnp.int32), counts.astype(jnp.int32))


def draw_queries(key, part):
    key = jax.random.fold_in(key, 5)
    full_matrix = jnp.clip(jax.random.normal(key, (SEQUENCE_COUNT, SEQUENCE_LENGTH, QUERY_HEADS, HEAD_SIZE), jnp.float32), -6.0, 6.0)
    return full_matrix.reshape(SEQUENCE_COUNT, SEQUENCE_LENGTH, QUERY_HEADS * HEAD_SIZE).astype(jnp.bfloat16)


def draw_keys(key, part):
    key = jax.random.fold_in(key, 7)
    full_matrix = jnp.clip(jax.random.normal(key, (SEQUENCE_COUNT, SEQUENCE_LENGTH, KEY_VALUE_HEADS, HEAD_SIZE), jnp.float32), -6.0, 6.0)
    return full_matrix.reshape(SEQUENCE_COUNT, SEQUENCE_LENGTH, KEY_VALUE_HEADS * HEAD_SIZE).astype(jnp.bfloat16)


def draw_key_blocks(key, part):
    picked, counts = block_plan(key)
    return picked


def draw_block_counts(key, part):
    picked, counts = block_plan(key)
    return counts


def block_scale(key, dims, pieces, least, top_value):
    def one(position, shards_of):
        draws = jax.random.uniform(jax.random.fold_in(jax.random.fold_in(key, 6), position), (shards_of,), jnp.float32, least / len(pieces), top_value / len(pieces))
        return jnp.repeat(jnp.exp(draws), dims[position] // shards_of).reshape((-1,) + (1,) * (len(dims) - position - 1))

    factor_of = one(*pieces[0])
    for cut in pieces[1:]:
        factor_of = factor_of * one(*cut)
    return factor_of


def profile(count, total, most, lean):
    portions = [(1 << 20) // math.isqrt(rank ** lean) + 1 for rank in range(2, count + 1)]
    rest, holding = total - most - (count - 1), [1] * (count - 1)
    while rest > 0:
        free = [i for i in range(count - 1) if holding[i] < most]
        mass, remaining = sum([portions[i] for i in free]), rest
        for i in free:
            extra = min(most - holding[i], max(1, remaining * portions[i] // mass), rest)
            holding[i] = holding[i] + extra
            rest = rest - extra
    return np.array([most] + holding)


def ragged(stream_key, amount, total, limit, skew):
    if amount == 2:
        one = jax.random.randint(stream_key, (), max(1, total - limit), min(limit, total - 1) + 1)
        return jnp.stack([one, total - one])
    sizes = jnp.asarray(profile(amount, total, limit, skew), jnp.int32)
    twos = (amount - 1) // 2
    donor, taker = sizes[1:1 + 2 * twos:2], sizes[2:2 + 2 * twos:2]
    margin = jnp.minimum(donor - 1, limit - taker)
    moved = jax.random.randint(jax.random.fold_in(stream_key, 1), (twos,), 0, 1 << 20) % (margin + 1)
    sizes = sizes.at[1:1 + 2 * twos:2].set(donor - moved).at[2:2 + 2 * twos:2].set(taker + moved)
    return sizes[jax.random.permutation(jax.random.fold_in(stream_key, 2), amount)]


def gaussian(rng, extent, deviation, bound, cuts=(), kind=jnp.bfloat16):
    gain = block_scale(rng, extent, cuts, -0.22, 0.18) if cuts else 1.0
    values = jax.random.normal(rng, extent, jnp.float32) * deviation * gain
    return jnp.minimum(jnp.maximum(values, -bound), bound).astype(kind)


def setup_inputs(seed: int = 0) -> dict:
    key_of = jax.random.split(jax.random.key(seed), 9)
    queries = draw_queries(jax.random.fold_in(key_of[8], 71), 0)
    keys = draw_keys(jax.random.fold_in(key_of[8], 71), 0)
    values = gaussian(key_of[2], (SEQUENCE_COUNT, SEQUENCE_LENGTH, KEY_VALUE_HEADS * HEAD_SIZE), 1.0, 6.0, ((0, 8), (1, 16)))
    key_blocks = draw_key_blocks(jax.random.fold_in(key_of[8], 71), 0)
    block_counts = draw_block_counts(jax.random.fold_in(key_of[8], 71), 0)
    doc_lengths = jax.vmap(lambda own: ragged(own, NDOC, SEQUENCE_LENGTH, SEQUENCE_LENGTH // 4, 2))(jax.random.split(key_of[5], SEQUENCE_COUNT)).reshape((SEQUENCE_COUNT, NDOC)).astype(jnp.int32)
    out_weight = gaussian(key_of[6], (QW, D), QW ** -0.5, 0.125, ((0, 16),))
    d_out = gaussian(key_of[7], (SEQUENCE_COUNT, SEQUENCE_LENGTH, D), 1.0, 6.0, ((0, 8), (1, 16)))
    return {"queries": queries, "keys": keys, "values": values, "key_blocks": key_blocks, "block_counts": block_counts, "doc_lengths": doc_lengths, "out_weight": out_weight, "d_out": d_out}


def doc_ids(lengths, count):
    starts = jnp.cumsum(lengths, dtype=jnp.int32) - lengths
    places = jnp.arange(count, dtype=jnp.int32)
    return lax.optimization_barrier(jnp.sum((places[:, None] >= starts[None, :]).astype(jnp.int32), axis=1, dtype=jnp.int32)) - 1

def block_mask(index, chosen, used, docs, width):
    slots = chosen.shape[0]
    query_pos = index * width + jnp.arange(width, dtype=jnp.int32)
    key_pos = (chosen[:, None] * width + jnp.arange(width, dtype=jnp.int32)[None, :]).reshape(slots * width)
    slot_ok = jnp.repeat(jnp.arange(slots, dtype=jnp.int32) < used, width)
    same_doc = docs[query_pos][:, None] == docs[key_pos][None, :]
    return slot_ok[None, :] & (key_pos[None, :] <= query_pos[:, None]) & same_doc

def head_forward(query, key_head, value_head, chosen_all, used_all, docs, scale):
    nblocks, slots = chosen_all.shape
    width = query.shape[0] // nblocks
    size = query.shape[1]
    query_blocks = query.reshape(nblocks, width, size)
    key_table = key_head.reshape(nblocks, width, size)
    value_table = value_head.reshape(nblocks, width, size)

    def one(index):
        chosen = chosen_all[index]
        rows_of_key = key_table[chosen].reshape(slots * width, size)
        value_rows = value_table[chosen].reshape(slots * width, size)
        mask = block_mask(index, chosen, used_all[index], docs, width)
        scores = jnp.dot(query_blocks[index], rows_of_key.T, preferred_element_type=jnp.float32) * scale
        scores = jnp.where(mask, scores, -jnp.inf)
        top = lax.optimization_barrier(jnp.max(scores, axis=1))
        weights = jnp.where(mask, jnp.exp(scores - top[:, None]), 0.0)
        total = lax.optimization_barrier(jnp.sum(weights, axis=1))
        probs = (weights / total[:, None]).astype(jnp.bfloat16)
        result = jnp.dot(probs, value_rows, preferred_element_type=jnp.float32).astype(jnp.bfloat16)
        return (result, top + jnp.log(total))
    results, log_total = lax.map(one, jnp.arange(nblocks, dtype=jnp.int32))
    return (results.reshape(nblocks * width, size), log_total.reshape(nblocks * width))

def head_backward(query, key_head, value_head, attn_head, grad_head, log_total, chosen_all, used_all, docs, scale):
    nblocks, slots = chosen_all.shape
    width = query.shape[0] // nblocks
    size = query.shape[1]
    query_blocks = query.reshape(nblocks, width, size)
    key_table = key_head.reshape(nblocks, width, size)
    value_table = value_head.reshape(nblocks, width, size)
    attn_blocks = attn_head.reshape(nblocks, width, size)
    grad_blocks = grad_head.reshape(nblocks, width, size)
    total_blocks = log_total.reshape(nblocks, width)

    def step(carry, index):
        sum_keys, sum_values = carry
        chosen = chosen_all[index]
        rows_of_key = key_table[chosen].reshape(slots * width, size)
        value_rows = value_table[chosen].reshape(slots * width, size)
        mask = block_mask(index, chosen, used_all[index], docs, width)
        scores = jnp.dot(query_blocks[index], rows_of_key.T, preferred_element_type=jnp.float32) * scale
        scores = jnp.where(mask, scores, -jnp.inf)
        back_probs = jnp.where(mask, jnp.exp(scores - total_blocks[index][:, None]), 0.0)
        back_round = back_probs.astype(jnp.bfloat16)
        grad_rows = grad_blocks[index]
        delta = lax.optimization_barrier(jnp.sum(grad_rows.astype(jnp.float32) * attn_blocks[index].astype(jnp.float32), axis=1))
        grad_p = jnp.dot(grad_rows, value_rows.T, preferred_element_type=jnp.float32)
        grad_scores = (back_probs * (grad_p - delta[:, None])).astype(jnp.bfloat16)
        grad_query = (jnp.dot(grad_scores, rows_of_key, preferred_element_type=jnp.float32) * scale).astype(jnp.bfloat16)
        part_keys = jnp.dot(grad_scores.T, query_blocks[index], preferred_element_type=jnp.float32).reshape(slots, width, size)
        part_values = jnp.dot(back_round.T, grad_rows, preferred_element_type=jnp.float32).reshape(slots, width, size)
        return ((sum_keys.at[chosen].add(part_keys), sum_values.at[chosen].add(part_values)), grad_query)
    start = (jnp.zeros((nblocks, width, size), jnp.float32), jnp.zeros((nblocks, width, size), jnp.float32))
    (sum_keys, sum_values), grad_query = lax.scan(step, start, jnp.arange(nblocks, dtype=jnp.int32))
    length = nblocks * width
    return (grad_query.reshape(length, size), sum_keys.reshape(length, size) * scale, sum_values.reshape(length, size))

def reference(queries, keys, values, key_blocks, block_counts, doc_lengths, out_weight, d_out):
    scale = 1.0 / math.sqrt(HEAD_SIZE)
    head_group = QUERY_HEADS // KEY_VALUE_HEADS

    def one_sequence(inputs):
        query, key_sequence, value_sequence, chosen, used, lengths, grad_out = inputs
        docs = doc_ids(lengths, SEQUENCE_LENGTH)
        query_heads = query.reshape(SEQUENCE_LENGTH, QUERY_HEADS, HEAD_SIZE).transpose(1, 0, 2)
        heads_of_key = key_sequence.reshape(SEQUENCE_LENGTH, KEY_VALUE_HEADS, HEAD_SIZE).transpose(1, 0, 2)
        heads_of_value = value_sequence.reshape(SEQUENCE_LENGTH, KEY_VALUE_HEADS, HEAD_SIZE).transpose(1, 0, 2)

        def forward(index):
            return head_forward(query_heads[index], heads_of_key[index // head_group], heads_of_value[index // head_group], chosen[index], used[index], docs, scale)
        attn_heads, log_total = lax.map(forward, jnp.arange(QUERY_HEADS, dtype=jnp.int32))
        attn = attn_heads.transpose(1, 0, 2).reshape(SEQUENCE_LENGTH, QUERY_HEADS * HEAD_SIZE)
        layer_out = jnp.dot(attn, out_weight, preferred_element_type=jnp.float32).astype(jnp.bfloat16)
        grad_attn = jnp.dot(grad_out, out_weight.T, preferred_element_type=jnp.float32).astype(jnp.bfloat16)
        grad_heads = grad_attn.reshape(SEQUENCE_LENGTH, QUERY_HEADS, HEAD_SIZE).transpose(1, 0, 2)

        def backward(index):
            return head_backward(query_heads[index], heads_of_key[index // head_group], heads_of_value[index // head_group], attn_heads[index], grad_heads[index], log_total[index], chosen[index], used[index], docs, scale)
        grad_q, key_gradient, value_gradient = lax.map(backward, jnp.arange(QUERY_HEADS, dtype=jnp.int32))
        grad_q = grad_q.transpose(1, 0, 2).reshape(SEQUENCE_LENGTH, QUERY_HEADS * HEAD_SIZE)
        key_gradient = lax.optimization_barrier(jnp.sum(key_gradient.reshape(KEY_VALUE_HEADS, head_group, SEQUENCE_LENGTH, HEAD_SIZE), axis=1)).astype(jnp.bfloat16)
        key_gradient = key_gradient.transpose(1, 0, 2).reshape(SEQUENCE_LENGTH, KEY_VALUE_HEADS * HEAD_SIZE)
        value_gradient = lax.optimization_barrier(jnp.sum(value_gradient.reshape(KEY_VALUE_HEADS, head_group, SEQUENCE_LENGTH, HEAD_SIZE), axis=1)).astype(jnp.bfloat16)
        value_gradient = value_gradient.transpose(1, 0, 2).reshape(SEQUENCE_LENGTH, KEY_VALUE_HEADS * HEAD_SIZE)
        attn_parts = attn.reshape(N_SP, TOK_DEV, QUERY_HEADS * HEAD_SIZE)
        grad_parts = grad_out.reshape(N_SP, TOK_DEV, D)

        def add_part(running, pair):
            part = jnp.dot(pair[0].T, pair[1], preferred_element_type=jnp.float32).astype(jnp.bfloat16)
            part = lax.optimization_barrier(part)
            return (running + part.astype(jnp.float32), None)
        weight_sum, _ = lax.scan(add_part, jnp.zeros((QUERY_HEADS * HEAD_SIZE, D), jnp.float32), (attn_parts, grad_parts))
        return (layer_out, grad_q, key_gradient, value_gradient, weight_sum)
    layer_out, grad_q, key_gradient, value_gradient, weight_sums = lax.map(one_sequence, (queries, keys, values, key_blocks, block_counts, doc_lengths, d_out))
    grad_weight = lax.optimization_barrier(jnp.sum(weight_sums, axis=0)) * (1.0 / math.sqrt(SEQUENCE_COUNT * SEQUENCE_LENGTH))
    return (layer_out, grad_q, key_gradient, value_gradient, grad_weight)
```

```python
import math

import jax
import jax.numpy as jnp
from jax import lax
from jax.experimental import pallas as pl
from jax.experimental.pallas import tpu as pltpu
from jax.sharding import PartitionSpec as P

SIZE = 128
TOK = 256
HALO = 4
BAND = (HALO + 1) * TOK
KB = BAND // SIZE
NEG = -1e30
BF = jnp.bfloat16
F32 = jnp.float32
NT = (((1,), (1,)), ((), ()))
TN = (((0,), (0,)), ((), ()))


def forward_body(q_ref, k_ref, v_ref, list_ref, bias_ref, attn_t_ref, attn_ref, p_ref, r_ref):
    scale = 1.0 / math.sqrt(SIZE)
    factor = scale * math.log2(math.e)
    for h in range(2):
        lanes = slice(h * SIZE, (h + 1) * SIZE)
        q = q_ref[:, lanes]
        tops = []
        scores = []
        for b in range(KB):
            rows = slice(b * SIZE, (b + 1) * SIZE)
            s = lax.dot_general(k_ref[rows, :], q, NT, preferred_element_type=F32)
            s = s + bias_ref[rows, :] + list_ref[h, b : b + 1, :]
            scores.append(s)
            tops.append(jnp.max(s, axis=0, keepdims=True))
        top = tops[0]
        for t in tops[1:]:
            top = jnp.maximum(top, t)
        total = jnp.zeros((1, TOK), F32)
        out = jnp.zeros((SIZE, TOK), F32)
        for b in range(KB):
            rows = slice(b * SIZE, (b + 1) * SIZE)
            p = jnp.exp2((scores[b] - top) * factor)
            total = total + jnp.sum(p, axis=0, keepdims=True)
            p_ref[h, rows, :] = p.astype(BF)
        out = lax.dot_general(v_ref[...], p_ref[h], TN, preferred_element_type=F32)
        inverse = 1.0 / total
        r_ref[h] = jnp.broadcast_to(inverse, (8, TOK))
        out = out * inverse
        attn_t_ref[lanes, :] = out.astype(BF)
        attn_ref[:, lanes] = out.T.astype(BF)


def forward_kernel(q_ref, k_ref, v_ref, list_ref, dq_ref, dk_ref, attn_t_ref, attn_ref, p_ref, r_ref, bias_ref):
    @pl.when(pl.program_id(0) == 0)
    def _():
        same = dk_ref[:, 0:1] == dq_ref[0:1, :]
        causal = dk_ref[:, 1:2] <= dq_ref[1:2, :]
        bias_ref[...] = jnp.where(same & causal, 0.0, NEG)

    forward_body(q_ref, k_ref, v_ref, list_ref, bias_ref, attn_t_ref, attn_ref, p_ref, r_ref)


def backward_kernel(q_ref, k_ref, v_ref, p_ref, r_ref, attn_t_ref, g_t_ref, dq_ref, dk_ref, dv_ref):
    scale = 1.0 / math.sqrt(SIZE)
    dk = jnp.zeros((BAND, SIZE), F32)
    dv = jnp.zeros((BAND, SIZE), F32)
    for h in range(2):
        lanes = slice(h * SIZE, (h + 1) * SIZE)
        inverse = r_ref[h, 0:1, :]
        g_t = g_t_ref[lanes, :].astype(F32)
        delta = jnp.sum(g_t * attn_t_ref[lanes, :].astype(F32), axis=0, keepdims=True) * inverse
        g_t = g_t * inverse
        g = g_t.T.astype(BF)
        dp = jnp.dot(v_ref[...], g_t.astype(BF), preferred_element_type=F32)
        p = p_ref[h]
        ds = (p.astype(F32) * (dp - delta)).astype(BF)
        dq_t = lax.dot_general(k_ref[...], ds, TN, preferred_element_type=F32)
        dq_ref[:, lanes] = (dq_t * scale).T.astype(BF)
        dk = dk + jnp.dot(ds, q_ref[:, lanes], preferred_element_type=F32)
        dv = dv + jnp.dot(p, g, preferred_element_type=F32)
    dk_ref[...] = (dk * scale).astype(BF)
    dv_ref[...] = dv.astype(BF)


def call_forward(q, k, v, lists, dq, dk):
    return pl.pallas_call(
        forward_kernel,
        grid=(8,),
        in_specs=[
            pl.BlockSpec((TOK, 2 * SIZE), lambda c: (0, c)),
            pl.BlockSpec((BAND, SIZE), lambda c: (0, c)),
            pl.BlockSpec((BAND, SIZE), lambda c: (0, c)),
            pl.BlockSpec((2, 16, TOK), lambda c: (c, 0, 0)),
            pl.BlockSpec((8, TOK), lambda c: (0, 0)),
            pl.BlockSpec((BAND, 2), lambda c: (0, 0)),
        ],
        out_specs=[
            pl.BlockSpec((2 * SIZE, TOK), lambda c: (c, 0)),
            pl.BlockSpec((TOK, 2 * SIZE), lambda c: (0, c)),
            pl.BlockSpec((2, BAND, TOK), lambda c: (c, 0, 0)),
            pl.BlockSpec((2, 8, TOK), lambda c: (c, 0, 0)),
        ],
        out_shape=[
            jax.ShapeDtypeStruct((2048, TOK), BF),
            jax.ShapeDtypeStruct((TOK, 2048), BF),
            jax.ShapeDtypeStruct((16, BAND, TOK), BF),
            jax.ShapeDtypeStruct((16, 8, TOK), F32),
        ],
        scratch_shapes=[pltpu.VMEM((BAND, TOK), F32)],
        compiler_params=pltpu.CompilerParams(vmem_limit_bytes=32 * 2**20),
        cost_estimate=pl.CostEstimate(flops=6 * 10**9, bytes_accessed=20 * 10**6, transcendentals=6 * 10**6),
    )(q, k, v, lists, dq, dk)


def call_backward(q, k, v, p, r, attn_t, g_t):
    return pl.pallas_call(
        backward_kernel,
        grid=(8,),
        in_specs=[
            pl.BlockSpec((TOK, 2 * SIZE), lambda c: (0, c)),
            pl.BlockSpec((BAND, SIZE), lambda c: (0, c)),
            pl.BlockSpec((BAND, SIZE), lambda c: (0, c)),
            pl.BlockSpec((2, BAND, TOK), lambda c: (c, 0, 0)),
            pl.BlockSpec((2, 8, TOK), lambda c: (c, 0, 0)),
            pl.BlockSpec((2 * SIZE, TOK), lambda c: (c, 0)),
            pl.BlockSpec((2 * SIZE, TOK), lambda c: (c, 0)),
        ],
        out_specs=[
            pl.BlockSpec((TOK, 2 * SIZE), lambda c: (0, c)),
            pl.BlockSpec((BAND, SIZE), lambda c: (0, c)),
            pl.BlockSpec((BAND, SIZE), lambda c: (0, c)),
        ],
        out_shape=[
            jax.ShapeDtypeStruct((TOK, 2048), BF),
            jax.ShapeDtypeStruct((BAND, 1024), BF),
            jax.ShapeDtypeStruct((BAND, 1024), BF),
        ],
        compiler_params=pltpu.CompilerParams(vmem_limit_bytes=32 * 2**20),
        cost_estimate=pl.CostEstimate(flops=10 * 10**9, bytes_accessed=30 * 10**6, transcendentals=0),
    )(q, k, v, p, r, attn_t, g_t)


def documents(positions, lengths):
    starts = jnp.cumsum(lengths, dtype=jnp.int32) - lengths
    return jnp.sum((positions[:, None] >= starts[None, :]).astype(jnp.int32), axis=1, dtype=jnp.int32) - 1


def list_terms(key_blocks, block_counts):
    slots = jnp.arange(8, dtype=jnp.int32)
    used = slots[None, :] < block_counts[:, None]
    device = jnp.arange(32, dtype=jnp.int32) // 2
    band = 2 * device[:, None] - 2 * HALO + jnp.arange(16, dtype=jnp.int32)[None, :]
    listed = jnp.any((key_blocks[:, None, :] == band[:, :, None]) & used[:, None, :], axis=2)
    term = jnp.where(listed, 0.0, NEG).astype(F32).reshape(16, 2, 16).transpose(0, 2, 1)
    return jnp.repeat(term, SIZE, axis=2)


def per_device(queries, keys, values, key_blocks, block_counts, doc_lengths, out_weight, d_out):
    q = queries[0]
    grad_out = d_out[0]
    me = lax.axis_index("sp")
    n = lax.axis_size("sp")
    piece = lax.all_gather(out_weight, "sp", axis=0, tiled=True)
    lists = lax.all_to_all(list_terms(key_blocks[0, 0], block_counts[0, 0]), "sp", split_axis=0, concat_axis=0, tiled=True)
    kv = jnp.concatenate([keys[0], values[0]], axis=1)
    parts = [lax.ppermute(kv, "sp", [(i, (i + s) % n) for i in range(n)]) for s in range(HALO, 0, -1)]
    band = jnp.concatenate(parts + [kv], axis=0)
    k, v = band[:, :1024], band[:, 1024:]
    q_pos = me * TOK + jnp.arange(TOK, dtype=jnp.int32)
    k_pos = (me - HALO) * TOK + jnp.arange(BAND, dtype=jnp.int32)
    dq = jnp.zeros((8, TOK), jnp.int32).at[0].set(documents(q_pos, doc_lengths[0])).at[1].set(q_pos)
    dk = jnp.stack([documents(k_pos, doc_lengths[0]), k_pos], axis=1)
    attn_t, attn, p, r = call_forward(q, k, v, lists, dq, dk)
    layer_out = jnp.dot(attn, piece, preferred_element_type=F32).astype(BF)
    g_t = lax.dot_general(piece, grad_out, NT, preferred_element_type=F32).astype(BF)
    weight_part = jnp.dot(attn_t, grad_out, preferred_element_type=F32).astype(BF)
    shard_rows = lax.psum_scatter(weight_part, "sp", scatter_dimension=0, tiled=True)
    summed = lax.psum(shard_rows, "dp").astype(F32)
    grad_weight = summed * (1.0 / math.sqrt(lax.axis_size("dp") * n * TOK))
    grad_q, dk_band, dv_band = call_backward(q, k, v, p, r, attn_t, g_t)
    dkv = jnp.concatenate([dk_band, dv_band], axis=1)
    total = dkv[HALO * TOK :].astype(F32)
    for s in range(HALO, 0, -1):
        piece_back = dkv[(HALO - s) * TOK : (HALO - s + 1) * TOK]
        back = lax.ppermute(piece_back, "sp", [(i, (i - s) % n) for i in range(n)])
        total = total + back.astype(F32)
    total = total.astype(BF)
    return (layer_out[None], grad_q[None], total[None, :, :1024], total[None, :, 1024:], grad_weight)


def solution(mesh):
    in_specs = (
        P("dp", "sp", None),
        P("dp", "sp", None),
        P("dp", "sp", None),
        P("dp", "sp", None, None),
        P("dp", "sp", None),
        P("dp", None),
        P("sp", None),
        P("dp", "sp", None),
    )
    out_specs = (
        P("dp", "sp", None),
        P("dp", "sp", None),
        P("dp", "sp", None),
        P("dp", "sp", None),
        P("sp", None),
    )
    return jax.shard_map(per_device, mesh=mesh, in_specs=in_specs, out_specs=out_specs, check_vma=False)
```

```python
import math

import jax
import jax.numpy as jnp
from jax import lax
from jax.experimental import pallas as pl
from jax.experimental.pallas import tpu as pltpu
from jax.sharding import PartitionSpec as P

SIZE = 128
TOK = 256
HALO = 4
BAND = (HALO + 1) * TOK
KB = BAND // SIZE
NEG = -1e30
BF = jnp.bfloat16
F32 = jnp.float32
NT = (((1,), (1,)), ((), ()))
TN = (((0,), (0,)), ((), ()))


def forward_body(q_ref, k_ref, v_ref, list_ref, bias_ref, attn_t_ref, attn_ref, p_ref, r_ref):
    scale = 1.0 / math.sqrt(SIZE)
    factor = scale * math.log2(math.e)
    for h in range(2):
        lanes = slice(h * SIZE, (h + 1) * SIZE)
        q = q_ref[:, lanes]
        tops = []
        scores = []
        for b in range(KB):
            rows = slice(b * SIZE, (b + 1) * SIZE)
            s = lax.dot_general(k_ref[rows, :], q, NT, preferred_element_type=F32)
            s = s + bias_ref[rows, :] + list_ref[h, b : b + 1, :]
            scores.append(s)
            tops.append(jnp.max(s, axis=0, keepdims=True))
        top = tops[0]
        for t in tops[1:]:
            top = jnp.maximum(top, t)
        total = jnp.zeros((1, TOK), F32)
        out = jnp.zeros((SIZE, TOK), F32)
        for b in range(KB):
            rows = slice(b * SIZE, (b + 1) * SIZE)
            p = jnp.exp2((scores[b] - top) * factor)
            total = total + jnp.sum(p, axis=0, keepdims=True)
            p_ref[h, rows, :] = p.astype(BF)
        out = lax.dot_general(v_ref[...], p_ref[h], TN, preferred_element_type=F32)
        inverse = 1.0 / total
        r_ref[h] = jnp.broadcast_to(inverse, (8, TOK))
        out = out * inverse
        attn_t_ref[lanes, :] = out.astype(BF)
        attn_ref[:, lanes] = out.T.astype(BF)


def forward_kernel(q_ref, k_ref, v_ref, list_ref, dq_ref, dk_ref, attn_t_ref, attn_ref, p_ref, r_ref, bias_ref):
    @pl.when(pl.program_id(0) == 0)
    def _():
        same = dk_ref[:, 0:1] == dq_ref[0:1, :]
        causal = dk_ref[:, 1:2] <= dq_ref[1:2, :]
        bias_ref[...] = jnp.where(same & causal, 0.0, NEG)

    forward_body(q_ref, k_ref, v_ref, list_ref, bias_ref, attn_t_ref, attn_ref, p_ref, r_ref)


def backward_kernel(q_ref, k_ref, v_ref, p_ref, r_ref, attn_t_ref, g_t_ref, dq_ref, dkv_ref):
    scale = 1.0 / math.sqrt(SIZE)
    dk = jnp.zeros((BAND, SIZE), F32)
    dv = jnp.zeros((BAND, SIZE), F32)
    for h in range(2):
        lanes = slice(h * SIZE, (h + 1) * SIZE)
        inverse = r_ref[h, 0:1, :]
        g_t = g_t_ref[lanes, :].astype(F32)
        delta = jnp.sum(g_t * attn_t_ref[lanes, :].astype(F32), axis=0, keepdims=True) * inverse
        g_t = g_t * inverse
        g = g_t.T.astype(BF)
        dp = jnp.dot(v_ref[...], g_t.astype(BF), preferred_element_type=F32)
        p = p_ref[h]
        ds = (p.astype(F32) * (dp - delta)).astype(BF)
        dq_t = lax.dot_general(k_ref[...], ds, TN, preferred_element_type=F32)
        dq_ref[:, lanes] = (dq_t * scale).T.astype(BF)
        dk = dk + jnp.dot(ds, q_ref[:, lanes], preferred_element_type=F32)
        dv = dv + jnp.dot(p, g, preferred_element_type=F32)
    dkv_ref[0] = (dk * scale).astype(BF)
    dkv_ref[1] = dv.astype(BF)


def call_forward(q, k, v, lists, dq, dk):
    return pl.pallas_call(
        forward_kernel,
        grid=(8,),
        in_specs=[
            pl.BlockSpec((TOK, 2 * SIZE), lambda c: (0, c)),
            pl.BlockSpec((BAND, SIZE), lambda c: (0, c)),
            pl.BlockSpec((BAND, SIZE), lambda c: (0, c)),
            pl.BlockSpec((2, 16, TOK), lambda c: (c, 0, 0)),
            pl.BlockSpec((8, TOK), lambda c: (0, 0)),
            pl.BlockSpec((BAND, 2), lambda c: (0, 0)),
        ],
        out_specs=[
            pl.BlockSpec((2 * SIZE, TOK), lambda c: (c, 0)),
            pl.BlockSpec((TOK, 2 * SIZE), lambda c: (0, c)),
            pl.BlockSpec((2, BAND, TOK), lambda c: (c, 0, 0)),
            pl.BlockSpec((2, 8, TOK), lambda c: (c, 0, 0)),
        ],
        out_shape=[
            jax.ShapeDtypeStruct((2048, TOK), BF),
            jax.ShapeDtypeStruct((TOK, 2048), BF),
            jax.ShapeDtypeStruct((16, BAND, TOK), BF),
            jax.ShapeDtypeStruct((16, 8, TOK), F32),
        ],
        scratch_shapes=[pltpu.VMEM((BAND, TOK), F32)],
        compiler_params=pltpu.CompilerParams(vmem_limit_bytes=32 * 2**20),
        cost_estimate=pl.CostEstimate(flops=6 * 10**9, bytes_accessed=20 * 10**6, transcendentals=6 * 10**6),
    )(q, k, v, lists, dq, dk)


def call_backward(q, k, v, p, r, attn_t, g_t):
    return pl.pallas_call(
        backward_kernel,
        grid=(8,),
        in_specs=[
            pl.BlockSpec((TOK, 2 * SIZE), lambda c: (0, c)),
            pl.BlockSpec((BAND, SIZE), lambda c: (0, c)),
            pl.BlockSpec((BAND, SIZE), lambda c: (0, c)),
            pl.BlockSpec((2, BAND, TOK), lambda c: (c, 0, 0)),
            pl.BlockSpec((2, 8, TOK), lambda c: (c, 0, 0)),
            pl.BlockSpec((2 * SIZE, TOK), lambda c: (c, 0)),
            pl.BlockSpec((2 * SIZE, TOK), lambda c: (c, 0)),
        ],
        out_specs=[
            pl.BlockSpec((TOK, 2 * SIZE), lambda c: (0, c)),
            pl.BlockSpec((2, BAND, SIZE), lambda c: (0, 0, c)),
        ],
        out_shape=[
            jax.ShapeDtypeStruct((TOK, 2048), BF),
            jax.ShapeDtypeStruct((2, BAND, 1024), BF),
        ],
        compiler_params=pltpu.CompilerParams(vmem_limit_bytes=32 * 2**20),
        cost_estimate=pl.CostEstimate(flops=10 * 10**9, bytes_accessed=30 * 10**6, transcendentals=0),
    )(q, k, v, p, r, attn_t, g_t)


def documents(positions, lengths):
    starts = jnp.cumsum(lengths, dtype=jnp.int32) - lengths
    return jnp.sum((positions[:, None] >= starts[None, :]).astype(jnp.int32), axis=1, dtype=jnp.int32) - 1


def list_terms(key_blocks, block_counts):
    slots = jnp.arange(8, dtype=jnp.int32)
    used = slots[None, :] < block_counts[:, None]
    device = jnp.arange(32, dtype=jnp.int32) // 2
    band = 2 * device[:, None] - 2 * HALO + jnp.arange(16, dtype=jnp.int32)[None, :]
    listed = jnp.any((key_blocks[:, None, :] == band[:, :, None]) & used[:, None, :], axis=2)
    term = jnp.where(listed, 0.0, NEG).astype(F32).reshape(16, 2, 16).transpose(0, 2, 1)
    return jnp.repeat(term, SIZE, axis=2)


MESH = pl.DeviceIdType.MESH
HALF = 1536
PART = 384


def place():
    dp = lax.axis_index("dp")
    sp = lax.axis_index("sp")
    return dp, sp, sp // 4, sp % 4


def sp_at(z, x):
    return (z + 4) % 4 * 4 + (x + 4) % 4


def dp_at(y, core):
    return (y + 4) % 4 * 2 + core


def greet():
    dp, sp, _, _ = place()
    barrier = pltpu.get_barrier_semaphore()
    for r in range(1, 16):
        pl.semaphore_signal(barrier, inc=1, device_id=(dp, (sp + r) % 16), device_id_type=MESH)
    for r in range(1, 8):
        pl.semaphore_signal(barrier, inc=1, device_id=((dp + r) % 8, sp), device_id_type=MESH)
    pl.semaphore_wait(barrier, 22)


def remote(src, dst, send, recv, dp, sp):
    return pltpu.make_async_remote_copy(
        src_ref=src, dst_ref=dst, send_sem=send, recv_sem=recv, device_id=(dp, sp), device_id_type=MESH
    )


class Sends:
    def __init__(self, sems):
        self.sems = sems
        self.started = []

    def go(self, src, dst, recv, dp, sp, when=None):
        copy = remote(src, dst, self.sems.at[len(self.started)], recv, dp, sp)
        self.started.append((copy, when))
        if when is None:
            copy.start()
        else:
            pl.when(when)(copy.start)

    def finish(self):
        for copy, when in self.started:
            if when is None:
                copy.wait_send()
            else:
                pl.when(when)(copy.wait_send)


def arrived(dst, recv):
    dp, sp, _, _ = place()
    remote(dst, dst, recv, recv, dp, sp).wait_recv()


def gather_kernel(
    k_ref, v_ref, lists_ref, w_ref, d_ref, kb_ref, vb_ref, lb_ref, wb_ref, db_ref, send, kv_recv, w_recv, pair_recv, l_recv, d_recv, local
):
    dp, sp, z, x = place()
    core = dp % 2
    other = dp + 1 - 2 * core
    cols = pl.ds(pl.multiple_of(core * HALF, HALF), HALF)
    part = lambda e: pl.ds(pl.multiple_of(e * PART, PART), PART)
    locals_ = [
        pltpu.make_async_copy(k_ref, kb_ref.at[4], local.at[0]),
        pltpu.make_async_copy(v_ref, vb_ref.at[4], local.at[1]),
        pltpu.make_async_copy(lists_ref.at[sp], lb_ref.at[sp], local.at[2]),
        pltpu.make_async_copy(w_ref, wb_ref.at[sp], local.at[3]),
        pltpu.make_async_copy(d_ref.at[:, part(dp)], db_ref.at[dp], local.at[4]),
    ]
    greet()
    out = Sends(send)

    def kv(which, src, slot, to, when=None):
        band = (kb_ref, vb_ref)[which]
        out.go(src, band.at[slot], kv_recv.at[which, slot], dp, to, when)

    own = (k_ref, v_ref)
    bands = (kb_ref, vb_ref)
    right, left = sp_at(z, x + 1), sp_at(z, x - 1)
    up, down = sp_at(z + 1, x), sp_at(z - 1, x)
    top, bottom = pl.ds(0, 64), pl.ds(64, 64)

    def weight(slot, rows, to):
        block = wb_ref.at[slot, rows, cols]
        out.go(block, block, w_recv.at[slot], dp, to)

    def weight_own(to):
        out.go(w_ref.at[:, cols], wb_ref.at[sp, :, cols], w_recv.at[sp], dp, to)

    def pair(slot):
        block = wb_ref.at[slot, :, cols]
        out.go(block, block, pair_recv.at[slot], other, sp)

    def weight_here(slot):
        arrived(wb_ref.at[slot, :, cols], w_recv.at[slot])

    weight_own(right)
    weight_own(left)
    for i in (0, 1):
        kv(i, own[i], 0, up)
    for i in (0, 1):
        kv(i, own[i], 3, right, x < 3)
        kv(i, own[i], 1, left, x == 0)
    weight_own(up)
    weight_own(down)
    for r in range(1, 16):
        to = (sp + r) % 16
        out.go(lists_ref.at[to], lb_ref.at[sp], l_recv, dp, to)
    for copy in locals_:
        copy.start()
    for r in range(1, 8):
        to = (dp + r) % 8
        out.go(d_ref.at[:, part(to)], db_ref.at[dp], d_recv, to, sp)

    whole = pl.ds(0, 128)
    a, b, c = sp_at(z, x - 1), sp_at(z, x + 1), sp_at(z, x + 2)
    weight_here(a)
    weight(a, top, right)
    weight(a, whole, up)
    weight(a, whole, down)
    weight_here(b)
    weight(b, bottom, left)
    weight(b, whole, up)
    weight(b, whole, down)
    pair(a)
    pair(b)
    for i in (0, 1):
        arrived(bands[i].at[0], kv_recv.at[i, 0])
        kv(i, bands[i].at[0], 3, right, x == 3)
        kv(i, bands[i].at[0], 1, left, x > 0)
    weight_here(c)
    weight(c, whole, up)
    weight(c, whole, down)
    pair(c)
    for i in (0, 1):
        arrived(bands[i].at[3], kv_recv.at[i, 3])
        kv(i, bands[i].at[3], 2, right, (x < 3) if i == 0 else (x == 2))
        arrived(bands[i].at[1], kv_recv.at[i, 1])
        kv(i, bands[i].at[1], 2, left, (x == 1) if i == 0 else (x > 0))
    for dx in (0, -1, 1, 2):
        below, above = sp_at(z - 1, x + dx), sp_at(z + 1, x + dx)
        weight_here(below)
        weight(below, top, up)
        pair(below)
        weight_here(above)
        weight(above, bottom, down)
        pair(above)
    for i in (0, 1):
        arrived(bands[i].at[2], kv_recv.at[i, 2])
    for dx in (0, -1, 1, 2):
        far = sp_at(z + 2, x + dx)
        weight_here(far)
        pair(far)
    for r in range(1, 16):
        slot = (sp + r) % 16
        arrived(wb_ref.at[slot, :, pl.ds(pl.multiple_of((1 - core) * HALF, HALF), HALF)], pair_recv.at[slot])
    arrived(lb_ref.at[pl.ds(0, 15)], l_recv)
    arrived(db_ref.at[pl.ds(0, 7)], d_recv)
    for copy in locals_:
        copy.wait()
    out.finish()


ANY = pl.BlockSpec(memory_space=pl.ANY)
DMA = pltpu.SemaphoreType.DMA


def call_gather(k, v, lists, w, d):
    return pl.pallas_call(
        gather_kernel,
        in_specs=[ANY] * 5,
        out_specs=[ANY] * 5,
        out_shape=[
            jax.ShapeDtypeStruct((5, TOK, 1024), BF),
            jax.ShapeDtypeStruct((5, TOK, 1024), BF),
            jax.ShapeDtypeStruct((16, 16, TOK), F32),
            jax.ShapeDtypeStruct((16, 128, 3072), BF),
            jax.ShapeDtypeStruct((8, TOK, PART), BF),
        ],
        scratch_shapes=[DMA((80,)), DMA((2, 5)), DMA((16,)), DMA((16,)), DMA, DMA, DMA((5,))],
        compiler_params=pltpu.CompilerParams(collective_id=0, has_side_effects=True),
    )(k, v, lists, w, d)


def spread_kernel(a_ref, ab_ref, send, recv, local):
    dp, sp, _, _ = place()
    y, core = dp // 2, dp % 2
    other = dp_at(y, 1 - core)
    copy = pltpu.make_async_copy(a_ref, ab_ref.at[dp], local)
    greet()
    out = Sends(send)
    copy.start()
    up, down = dp_at(y + 1, core), dp_at(y - 1, core)
    far = dp_at(y + 2, core)
    out.go(a_ref, ab_ref.at[dp], recv.at[dp], up, sp)
    out.go(a_ref, ab_ref.at[dp], recv.at[dp], down, sp)
    out.go(a_ref, ab_ref.at[dp], recv.at[dp], other, sp)

    def on(slot, rows, to):
        block = ab_ref.at[slot, rows]
        out.go(block, block, recv.at[slot], to, sp)

    for slot, rows, to in ((down, pl.ds(0, 1024), up), (up, pl.ds(1024, 1024), down)):
        arrived(ab_ref.at[slot], recv.at[slot])
        on(slot, rows, to)
        on(slot, pl.ds(0, 2048), other)
    arrived(ab_ref.at[far], recv.at[far])
    on(far, pl.ds(0, 2048), other)
    for r in range(4):
        slot = dp_at(y + r, 1 - core)
        arrived(ab_ref.at[slot], recv.at[slot])
    copy.wait()
    out.finish()


def call_spread(attn_t):
    return pl.pallas_call(
        spread_kernel,
        in_specs=[ANY],
        out_specs=ANY,
        out_shape=jax.ShapeDtypeStruct((8, 2048, TOK), BF),
        scratch_shapes=[DMA((8,)), DMA((8,)), DMA],
        compiler_params=pltpu.CompilerParams(collective_id=1, has_side_effects=True),
    )(attn_t)


def return_kernel(g_ref, b_ref, gb_ref, o_ref, rs, back, low, mine, gsum, send, rs_recv, g_recv, row_recv, z_recv, local):
    dp, sp, z, x = place()
    loads = [
        pltpu.make_async_copy(g_ref.at[sp], rs.at[sp], local.at[0]),
        pltpu.make_async_copy(b_ref.at[:, 0], low, local.at[1]),
        pltpu.make_async_copy(b_ref.at[:, 4], mine, local.at[2]),
    ]
    greet()
    out = Sends(send)
    for copy in loads:
        copy.start()
    for k in (2, 1, 3):
        out.go(b_ref.at[:, 4 - k], back.at[k - 1], row_recv.at[k - 1], dp, sp_at(z, x - k))
    for r in range(1, 16):
        to = (sp + r) % 16
        out.go(g_ref.at[to], rs.at[sp], rs_recv, dp, to)
    for copy in loads:
        copy.wait()
    arrived(rs.at[pl.ds(0, 15)], rs_recv)
    total = rs[0].astype(F32)
    for i in range(1, 16):
        total = total + rs[i].astype(F32)
    gsum[...] = total.astype(BF)
    for r in range(1, 8):
        out.go(gsum, gb_ref.at[dp], g_recv, (dp + r) % 8, sp)
    final = pltpu.make_async_copy(gsum, gb_ref.at[dp], local.at[3])
    final.start()
    for k in (1, 2, 3):
        arrived(back.at[k - 1], row_recv.at[k - 1])
    keep = [jnp.where(x + k < 4, 1.0, 0.0).astype(F32) for k in (1, 2, 3)]

    def rows_of(i):
        return pl.ds(pl.multiple_of(i * 32, 32), 32)

    def add(i, _):
        w, rows = i // 8, rows_of(i % 8)
        below = low[w, rows].astype(F32)
        here = mine[w, rows].astype(F32)
        for k in range(3):
            got = back[k, w, rows].astype(F32)
            here = here + got * keep[k]
            below = below + got * (1.0 - keep[k])
        low[w, rows] = below.astype(BF)
        mine[w, rows] = here.astype(BF)
        return 0

    lax.fori_loop(0, 16, add, 0)
    out.go(low, back.at[3], z_recv, dp, sp_at(z - 1, x))
    arrived(gb_ref.at[pl.ds(0, 7)], g_recv)
    final.wait()
    arrived(back.at[3], z_recv)

    def last(i, _):
        w, rows = i // 8, rows_of(i % 8)
        o_ref[w, rows] = (mine[w, rows].astype(F32) + back[3, w, rows].astype(F32)).astype(BF)
        return 0

    lax.fori_loop(0, 16, last, 0)
    out.finish()


def call_return(g, bands):
    vmem = pl.BlockSpec(memory_space=pltpu.VMEM)
    return pl.pallas_call(
        return_kernel,
        in_specs=[ANY, ANY],
        out_specs=[ANY, vmem],
        out_shape=[
            jax.ShapeDtypeStruct((8, 128, PART), BF),
            jax.ShapeDtypeStruct((2, TOK, 1024), BF),
        ],
        scratch_shapes=[
            pltpu.VMEM((16, 128, PART), BF),
            pltpu.VMEM((4, 2, TOK, 1024), BF),
            pltpu.VMEM((2, TOK, 1024), BF),
            pltpu.VMEM((2, TOK, 1024), BF),
            pltpu.VMEM((128, PART), BF),
            DMA((32,)),
            DMA,
            DMA,
            DMA((3,)),
            DMA,
            DMA((4,)),
        ],
        compiler_params=pltpu.CompilerParams(collective_id=2, has_side_effects=True, vmem_limit_bytes=32 * 2**20),
    )(g, bands)


def per_device(queries, keys, values, key_blocks, block_counts, doc_lengths, out_weight, d_out):
    q = queries[0]
    grad_out = d_out[0]
    me = lax.axis_index("sp")
    n = lax.axis_size("sp")
    lists = list_terms(key_blocks[0, 0], block_counts[0, 0])
    k, v, lists, weight, grad_parts = call_gather(keys[0], values[0], lists, out_weight, grad_out)
    k = k.reshape(BAND, 1024)
    v = v.reshape(BAND, 1024)
    weight = weight.reshape(2048, 3072)
    q_pos = me * TOK + jnp.arange(TOK, dtype=jnp.int32)
    k_pos = (me - HALO) * TOK + jnp.arange(BAND, dtype=jnp.int32)
    dq = jnp.zeros((8, TOK), jnp.int32).at[0].set(documents(q_pos, doc_lengths[0])).at[1].set(q_pos)
    dk = jnp.stack([documents(k_pos, doc_lengths[0]), k_pos], axis=1)
    attn_t, attn, p, r = call_forward(q, k, v, lists, dq, dk)
    attn_all = call_spread(attn_t)
    g_t = lax.dot_general(weight, grad_out, NT, preferred_element_type=F32).astype(BF)
    grad_q, bands = call_backward(q, k, v, p, r, attn_t, g_t)
    weight_part = lax.dot_general(
        attn_all, grad_parts, (((0, 2), (0, 1)), ((), ())), preferred_element_type=F32
    ).astype(BF)
    grad_all, grad_kv = call_return(weight_part.reshape(16, 128, PART), bands.reshape(2, 5, TOK, 1024))
    layer_out = jnp.dot(attn, weight, preferred_element_type=F32).astype(BF)
    grad_weight = grad_all.transpose(1, 0, 2).reshape(128, 3072).astype(F32)
    grad_weight = grad_weight * (1.0 / math.sqrt(lax.axis_size("dp") * n * TOK))
    return (layer_out[None], grad_q[None], grad_kv[:1], grad_kv[1:], grad_weight)


def solution(mesh):
    in_specs = (
        P("dp", "sp", None),
        P("dp", "sp", None),
        P("dp", "sp", None),
        P("dp", "sp", None, None),
        P("dp", "sp", None),
        P("dp", None),
        P("sp", None),
        P("dp", "sp", None),
    )
    out_specs = (
        P("dp", "sp", None),
        P("dp", "sp", None),
        P("dp", "sp", None),
        P("dp", "sp", None),
        P("sp", None),
    )
    return jax.shard_map(per_device, mesh=mesh, in_specs=in_specs, out_specs=out_specs, check_vma=False)
```

```python
import math

import jax
import jax.numpy as jnp
from jax import lax
from jax.experimental import pallas as pl
from jax.experimental.pallas import tpu as pltpu
from jax.sharding import PartitionSpec as P

SIZE = 128
TOK = 256
HALO = 4
BAND = (HALO + 1) * TOK
KB = BAND // SIZE
NEG = -1e30
BF = jnp.bfloat16
F32 = jnp.float32
NT = (((1,), (1,)), ((), ()))
TN = (((0,), (0,)), ((), ()))


def list_terms(key_blocks, block_counts):
    slots = jnp.arange(8, dtype=jnp.int32)
    used = slots[None, :] < block_counts[:, None]
    device = jnp.arange(32, dtype=jnp.int32) // 2
    band = 2 * device[:, None] - 2 * HALO + jnp.arange(16, dtype=jnp.int32)[None, :]
    listed = jnp.any((key_blocks[:, None, :] == band[:, :, None]) & used[:, None, :], axis=2)
    term = jnp.where(listed, 0.0, NEG).astype(F32).reshape(16, 2, 16).transpose(0, 2, 1)
    return jnp.repeat(term, SIZE, axis=2)


MESH = pl.DeviceIdType.MESH
HALF = 1536
PART = 384


def place():
    dp = lax.axis_index("dp")
    sp = lax.axis_index("sp")
    return dp, sp, sp // 4, sp % 4


def sp_at(z, x):
    return (z + 4) % 4 * 4 + (x + 4) % 4


def dp_at(y, core):
    return (y + 4) % 4 * 2 + core


def greet():
    dp, sp, _, _ = place()
    barrier = pltpu.get_barrier_semaphore()
    for r in range(1, 16):
        pl.semaphore_signal(barrier, inc=1, device_id=(dp, (sp + r) % 16), device_id_type=MESH)
    for r in range(1, 8):
        pl.semaphore_signal(barrier, inc=1, device_id=((dp + r) % 8, sp), device_id_type=MESH)
    pl.semaphore_wait(barrier, 22)


def remote(src, dst, send, recv, dp, sp):
    return pltpu.make_async_remote_copy(
        src_ref=src, dst_ref=dst, send_sem=send, recv_sem=recv, device_id=(dp, sp), device_id_type=MESH
    )


class Sends:
    def __init__(self, sems):
        self.sems = sems
        self.started = []

    def go(self, src, dst, recv, dp, sp, when=None):
        copy = remote(src, dst, self.sems.at[len(self.started)], recv, dp, sp)
        self.started.append((copy, when))
        if when is None:
            copy.start()
        else:
            pl.when(when)(copy.start)

    def finish(self):
        for copy, when in self.started:
            if when is None:
                copy.wait_send()
            else:
                pl.when(when)(copy.wait_send)


def arrived(dst, recv):
    dp, sp, _, _ = place()
    remote(dst, dst, recv, recv, dp, sp).wait_recv()


SCALE = 1.0 / math.sqrt(SIZE)
FACTOR = SCALE * math.log2(math.e)
ANY = pl.BlockSpec(memory_space=pl.ANY)
DMA = pltpu.SemaphoreType.DMA


def lanes_of(i, width):
    return pl.ds(pl.multiple_of(i * width, width), width)


def forward_heads(c, qs, band, lb, bias, pb, rb, aa, an, dp):
    cols = lanes_of(c, SIZE)
    for h in range(2):
        head = 2 * c + h
        lanes = lanes_of(head, SIZE)
        q = qs[:, lanes]
        scores = []
        top = None
        for b in range(KB):
            k = band[0, b // 2, pl.ds(b % 2 * SIZE, SIZE), cols]
            s = lax.dot_general(k, q, NT, preferred_element_type=F32)
            s = s + bias[b * SIZE : (b + 1) * SIZE, :] + lb[head, b : b + 1, :]
            scores.append(s)
            t = jnp.max(s, axis=0, keepdims=True)
            top = t if top is None else jnp.maximum(top, t)
        total = jnp.zeros((1, TOK), F32)
        for b in range(KB):
            p = jnp.exp2((scores[b] - top) * FACTOR)
            total = total + jnp.sum(p, axis=0, keepdims=True)
            pb[head, b * SIZE : (b + 1) * SIZE, :] = p.astype(BF)
        v = band[1, :, :, cols].reshape(BAND, SIZE)
        out = lax.dot_general(v, pb[head], TN, preferred_element_type=F32)
        inverse = 1.0 / total
        rb[head] = jnp.broadcast_to(inverse, (8, TOK))
        out = out * inverse
        aa[dp, lanes, :] = out.astype(BF)
        an[:, lanes] = out.T.astype(BF)


def backward_heads(c, qs, band, pb, rb, aa, gt, dp):
    cols = lanes_of(c, SIZE)
    k = band[0, :, :, cols].reshape(BAND, SIZE)
    v = band[1, :, :, cols].reshape(BAND, SIZE)
    dk = jnp.zeros((BAND, SIZE), F32)
    dv = jnp.zeros((BAND, SIZE), F32)
    for h in range(2):
        head = 2 * c + h
        lanes = lanes_of(head, SIZE)
        inverse = rb[head, 0:1, :]
        g_t = gt[lanes, :].astype(F32)
        delta = jnp.sum(g_t * aa[dp, lanes, :].astype(F32), axis=0, keepdims=True) * inverse
        g_t = g_t * inverse
        g = g_t.T.astype(BF)
        grad_p = jnp.dot(v, g_t.astype(BF), preferred_element_type=F32)
        p = pb[head]
        grad_s = (p.astype(F32) * (grad_p - delta)).astype(BF)
        dq_t = lax.dot_general(k, grad_s, TN, preferred_element_type=F32)
        dk = dk + jnp.dot(grad_s, qs[:, lanes], preferred_element_type=F32)
        dv = dv + jnp.dot(p, g, preferred_element_type=F32)
        qs[:, lanes] = (dq_t * SCALE).T.astype(BF)
    band[0, :, :, cols] = (dk * SCALE).astype(BF).reshape(5, TOK, SIZE)
    band[1, :, :, cols] = dv.astype(BF).reshape(5, TOK, SIZE)


def layer_kernel(
    q_ref, k_ref, v_ref, lists_ref, len_ref, w_ref, d_ref,
    lo_ref, dq_ref, gkv_ref, gb_ref,
    band, lb, wb, db, qs, ds, bias, pb, rb, aa, an, gt, back, gw, rs, gsum,
    local, kv_send, kv_recv, w_send, w_recv, relay_send, pair_send, pair_recv, first_send, l_recv, d_recv,
    a_send, a_recv, a_relay, row_send, row_recv, z_send, z_recv, rs_send, rs_recv, g_send, g_recv,
):
    dp, sp, z, x = place()
    y, core = dp // 2, dp % 2
    other = dp_at(y, 1 - core)
    half = lanes_of(core, HALF)
    loads = [
        pltpu.make_async_copy(k_ref, band.at[0, 4], local.at[0]),
        pltpu.make_async_copy(v_ref, band.at[1, 4], local.at[1]),
        pltpu.make_async_copy(lists_ref.at[sp], lb.at[sp], local.at[2]),
        pltpu.make_async_copy(w_ref, wb.at[sp], local.at[3]),
        pltpu.make_async_copy(d_ref.at[:, lanes_of(dp, PART)], db.at[dp], local.at[4]),
        pltpu.make_async_copy(q_ref, qs, local.at[5]),
        pltpu.make_async_copy(d_ref, ds, local.at[6]),
    ]
    for copy in loads:
        copy.start()
    greet()
    kv_out, w_out, first_out = Sends(kv_send), Sends(w_send), Sends(first_send)
    own = (k_ref, v_ref)
    right, left = sp_at(z, x + 1), sp_at(z, x - 1)
    up, down = sp_at(z + 1, x), sp_at(z - 1, x)
    top, bottom = pl.ds(0, 64), pl.ds(64, 64)

    def kv(i, src, slot, to, when=None):
        kv_out.go(src, band.at[i, slot], kv_recv.at[i, slot], dp, to, when)

    def kv_here(i, slot):
        arrived(band.at[i, slot], kv_recv.at[i, slot])

    def weight(slot, rows, to):
        block = wb.at[slot, rows, half]
        w_out.go(block, block, w_recv.at[slot], dp, to)

    def weight_own(to):
        w_out.go(w_ref.at[:, half], wb.at[sp, :, half], w_recv.at[sp], dp, to)

    def weight_here(slot):
        arrived(wb.at[slot, :, half], w_recv.at[slot])

    def pair(slot):
        block = wb.at[slot, :, half]
        return remote(block, block, pair_send.at[slot], pair_recv.at[slot], other, sp)

    weight_own(right)
    weight_own(left)
    for i in (0, 1):
        kv(i, own[i], 0, up)
    for i in (0, 1):
        kv(i, own[i], 3, right, x < 3)
        kv(i, own[i], 1, left, x == 0)
    for r in range(1, 16):
        to = (sp + r) % 16
        first_out.go(lists_ref.at[to], lb.at[sp], l_recv, dp, to)
    weight_own(up)
    weight_own(down)
    for r in range(1, 8):
        to = (dp + r) % 8
        first_out.go(d_ref.at[:, lanes_of(to, PART)], db.at[dp], d_recv, to, sp)

    q_pos = sp * TOK + lax.broadcasted_iota(jnp.int32, (1, TOK), 1)
    begin = jnp.zeros((1, TOK), jnp.int32)
    start = jnp.int32(0)
    for i in range(16):
        begin = jnp.where(q_pos >= start, start, begin)
        start = start + len_ref[0, i]

    def mask(b, _):
        rows = pl.ds(pl.multiple_of(b * SIZE, SIZE), SIZE)
        k_pos = (sp - HALO) * TOK + b * SIZE + lax.broadcasted_iota(jnp.int32, (SIZE, TOK), 0)
        bias[rows, :] = jnp.where((k_pos <= q_pos) & (k_pos >= begin), 0.0, NEG)
        return 0

    lax.fori_loop(0, KB, mask, 0)

    whole = pl.ds(0, 128)
    a, b, c2 = left, right, sp_at(z, x + 2)
    weight_here(a)
    weight(a, top, right)
    weight(a, whole, up)
    weight(a, whole, down)
    weight_here(b)
    weight(b, bottom, left)
    weight(b, whole, up)
    weight(b, whole, down)
    pair(a).start()
    pair(b).start()
    for i in (0, 1):
        kv_here(i, 0)
        kv(i, band.at[i, 0], 3, right, x == 3)
        kv(i, band.at[i, 0], 1, left, x > 0)
    weight_here(c2)
    weight(c2, whole, up)
    weight(c2, whole, down)
    pair(c2).start()
    for i in (0, 1):
        kv_here(i, 3)
        kv(i, band.at[i, 3], 2, right, (x < 3) if i == 0 else (x == 2))
        kv_here(i, 1)
        kv(i, band.at[i, 1], 2, left, (x == 1) if i == 0 else (x > 0))
    for i in (0, 1):
        kv_here(i, 2)
    arrived(lb.at[pl.ds(0, 15)], l_recv)
    for copy in loads:
        copy.wait()

    def relay(i):
        above = i % 2
        slot = sp_at(z - 1 + 2 * above, x + i // 2)
        block = wb.at[slot, pl.ds(pl.multiple_of(above * 64, 64), 64), half]
        return slot, remote(block, block, relay_send.at[i], w_recv.at[slot], dp, sp_at(z + 1 - 2 * above, x))

    y_up, y_down, y_far = dp_at(y + 1, core), dp_at(y - 1, core), dp_at(y + 2, core)

    def forward(c, _):
        forward_heads(c, qs, band, lb, bias, pb, rb, aa, an, dp)
        rows = pl.ds(pl.multiple_of(c * TOK, TOK), TOK)
        block = aa.at[dp, rows]
        for i, to in enumerate((y_up, y_down, other)):
            remote(block, block, a_send.at[i], a_recv.at[dp], to, sp).start()
        slot, copy = relay(c)
        weight_here(slot)
        copy.start()
        pair(slot).start()
        return 0

    lax.fori_loop(0, 8, forward, 0)

    def far(i, _):
        slot = sp_at(z + 2, x + i)
        weight_here(slot)
        pair(slot).start()
        return 0

    lax.fori_loop(0, 4, far, 0)
    other_half = lanes_of(1 - core, HALF)

    def pairs(r, _):
        slot = (sp + r) % 16
        arrived(wb.at[slot, :, other_half], pair_recv.at[slot])
        return 0

    lax.fori_loop(1, 16, pairs, 0)

    def grad_attn(i, _):
        w = wb[pl.ds(2 * i, 2)].reshape(TOK, 3072)
        g = lax.dot_general(w, ds[...], NT, preferred_element_type=F32)
        gt[pl.ds(pl.multiple_of(i * TOK, TOK), TOK), :] = g.astype(BF)
        return 0

    lax.fori_loop(0, 8, grad_attn, 0)

    a_out = Sends(a_relay)

    def on(slot, rows, to):
        block = aa.at[slot, rows]
        a_out.go(block, block, a_recv.at[slot], to, sp)

    for slot, rows, to in ((y_down, pl.ds(0, 1024), y_up), (y_up, pl.ds(1024, 1024), y_down)):
        arrived(aa.at[slot], a_recv.at[slot])
        on(slot, rows, to)
        on(slot, pl.ds(0, 2048), other)
    kv_out.finish()

    def backward(c, _):
        backward_heads(c, qs, band, pb, rb, aa, gt, dp)
        cols = lanes_of(c, SIZE)
        for k in (2, 1, 3):
            remote(
                band.at[:, 4 - k, :, cols], back.at[k - 1, :, :, cols], row_send.at[k - 1], row_recv.at[k - 1, c], dp, sp_at(z, x - k)
            ).start()
        return 0

    lax.fori_loop(0, 8, backward, 0)
    dq_out = pltpu.make_async_copy(qs, dq_ref, local.at[7])
    dq_out.start()
    arrived(aa.at[y_far], a_recv.at[y_far])
    on(y_far, pl.ds(0, 2048), other)
    for r in range(4):
        slot = dp_at(y + r, 1 - core)
        arrived(aa.at[slot], a_recv.at[slot])
    arrived(db.at[pl.ds(0, 7)], d_recv)

    def weight_grad(t, _):
        j = (z + t) % 4
        rows = pl.ds(pl.multiple_of(j * 512, 512), 512)
        total = jnp.zeros((512, PART), F32)
        for e in range(8):
            total = total + jnp.dot(aa[e, rows, :], db[e], preferred_element_type=F32)
        gw[pl.ds(4 * j, 4)] = total.astype(BF).reshape(4, 128, PART)
        for i in range(4):
            to = 4 * j + (x + i) % 4

            @pl.when(to != sp)
            def _():
                remote(gw.at[to], rs.at[sp], rs_send, rs_recv, dp, to).start()

        return 0

    lax.fori_loop(0, 4, weight_grad, 0)

    keep = [jnp.where(x + k < 4, 1.0, 0.0).astype(F32) for k in (1, 2, 3)]

    def z_copy(c):
        cols = lanes_of(c, SIZE)
        return remote(band.at[:, 0, :, cols], back.at[3, :, :, cols], z_send, z_recv.at[c], dp, down)

    def row_sums(c, _):
        cols = lanes_of(c, SIZE)
        for k in range(3):
            arrived(back.at[k, :, :, cols], row_recv.at[k, c])
        below = band[:, 0, :, cols].astype(F32)
        here = band[:, 4, :, cols].astype(F32)
        for k in range(3):
            got = back[k, :, :, cols].astype(F32)
            here = here + got * keep[k]
            below = below + got * (1.0 - keep[k])
        band[:, 0, :, cols] = below.astype(BF)
        band[:, 4, :, cols] = here.astype(BF)
        z_copy(c).start()
        return 0

    lax.fori_loop(0, 8, row_sums, 0)

    def project(i, _):
        cols = lanes_of(i, 512)
        w = wb[:, :, cols].reshape(2048, 512)
        ds[:, cols] = jnp.dot(an[...], w, preferred_element_type=F32).astype(BF)
        return 0

    lax.fori_loop(0, 6, project, 0)
    lo_out = pltpu.make_async_copy(ds, lo_ref, local.at[8])
    lo_out.start()

    arrived(rs.at[pl.ds(0, 15)], rs_recv)
    total = gw[sp].astype(F32)
    for r in range(1, 16):
        total = total + rs[(sp + r) % 16].astype(F32)
    gsum[...] = total.astype(BF)
    g_out = Sends(g_send)
    for r in range(1, 8):
        g_out.go(gsum, gb_ref.at[dp], g_recv, (dp + r) % 8, sp)
    own_sum = pltpu.make_async_copy(gsum, gb_ref.at[dp], local.at[9])
    own_sum.start()

    def last(c, _):
        cols = lanes_of(c, SIZE)
        arrived(back.at[3, :, :, cols], z_recv.at[c])
        here = band[:, 4, :, cols].astype(F32) + back[3, :, :, cols].astype(F32)
        band[:, 4, :, cols] = here.astype(BF)
        return 0

    lax.fori_loop(0, 8, last, 0)
    gkv_out = pltpu.make_async_copy(band.at[:, 4], gkv_ref, local.at[10])
    gkv_out.start()

    w_out.finish()
    first_out.finish()
    a_out.finish()

    def relays(i, _):
        relay(i)[1].wait_send()
        return 0

    lax.fori_loop(0, 8, relays, 0)

    def pairs_sent(r, _):
        pair((sp + r) % 16).wait_send()
        return 0

    lax.fori_loop(1, 16, pairs_sent, 0)
    for i in range(3):
        remote(aa.at[dp], aa.at[dp], a_send.at[i], a_recv.at[dp], other, sp).wait_send()
    for k in range(3):
        remote(back.at[k], back.at[k], row_send.at[k], row_send.at[k], dp, left).wait_send()
    remote(back.at[3], back.at[3], z_send, z_send, dp, down).wait_send()
    remote(rs.at[pl.ds(0, 15)], rs.at[pl.ds(0, 15)], rs_send, rs_send, dp, left).wait_send()
    arrived(gb_ref.at[pl.ds(0, 7)], g_recv)
    g_out.finish()
    for copy in (dq_out, lo_out, own_sum, gkv_out):
        copy.wait()


def call_layer(q, k, v, lists, lengths, w, d):
    vmem = pltpu.VMEM
    return pl.pallas_call(
        layer_kernel,
        in_specs=[ANY] * 4 + [pl.BlockSpec(memory_space=pltpu.SMEM)] + [ANY] * 2,
        out_specs=[ANY] * 4,
        out_shape=[
            jax.ShapeDtypeStruct((TOK, 3072), BF),
            jax.ShapeDtypeStruct((TOK, 2048), BF),
            jax.ShapeDtypeStruct((2, TOK, 1024), BF),
            jax.ShapeDtypeStruct((8, 128, PART), BF),
        ],
        scratch_shapes=[
            vmem((2, 5, TOK, 1024), BF),
            vmem((16, 16, TOK), F32),
            vmem((16, 128, 3072), BF),
            vmem((8, TOK, PART), BF),
            vmem((TOK, 2048), BF),
            vmem((TOK, 3072), BF),
            vmem((BAND, TOK), F32),
            vmem((16, BAND, TOK), BF),
            vmem((16, 8, TOK), F32),
            vmem((8, 2048, TOK), BF),
            vmem((TOK, 2048), BF),
            vmem((2048, TOK), BF),
            vmem((4, 2, TOK, 1024), BF),
            vmem((16, 128, PART), BF),
            vmem((16, 128, PART), BF),
            vmem((128, PART), BF),
            DMA((11,)),
            DMA((16,)),
            DMA((2, 5)),
            DMA((12,)),
            DMA((16,)),
            DMA((8,)),
            DMA((16,)),
            DMA((16,)),
            DMA((22,)),
            DMA,
            DMA,
            DMA((3,)),
            DMA((8,)),
            DMA((5,)),
            DMA((3,)),
            DMA((3, 8)),
            DMA,
            DMA((8,)),
            DMA,
            DMA,
            DMA((7,)),
            DMA,
        ],
        compiler_params=pltpu.CompilerParams(collective_id=0, has_side_effects=True, vmem_limit_bytes=60 * 2**20),
        cost_estimate=pl.CostEstimate(flops=27 * 10**9, bytes_accessed=20 * 10**6, transcendentals=6 * 10**6),
    )(q, k, v, lists, lengths, w, d)


def per_device(queries, keys, values, key_blocks, block_counts, doc_lengths, out_weight, d_out):
    lists = list_terms(key_blocks[0, 0], block_counts[0, 0])
    layer_out, grad_q, grad_kv, grad_all = call_layer(
        queries[0], keys[0], values[0], lists, doc_lengths, out_weight, d_out[0]
    )
    grad_weight = grad_all.transpose(1, 0, 2).reshape(128, 3072).astype(F32)
    tokens = lax.axis_size("dp") * lax.axis_size("sp") * TOK
    grad_weight = grad_weight * (1.0 / math.sqrt(tokens))
    return (layer_out[None], grad_q[None], grad_kv[:1], grad_kv[1:], grad_weight)


def solution(mesh):
    in_specs = (
        P("dp", "sp", None),
        P("dp", "sp", None),
        P("dp", "sp", None),
        P("dp", "sp", None, None),
        P("dp", "sp", None),
        P("dp", None),
        P("sp", None),
        P("dp", "sp", None),
    )
    out_specs = (
        P("dp", "sp", None),
        P("dp", "sp", None),
        P("dp", "sp", None),
        P("dp", "sp", None),
        P("sp", None),
    )
    return jax.shard_map(per_device, mesh=mesh, in_specs=in_specs, out_specs=out_specs, check_vma=False)
```

```python
import math

import jax
import jax.numpy as jnp
from jax import lax
from jax.experimental import pallas as pl
from jax.experimental.pallas import tpu as pltpu
from jax.sharding import PartitionSpec as P

SIZE = 128
TOK = 256
HALO = 4
BAND = (HALO + 1) * TOK
KB = BAND // SIZE
NEG = -1e30
BF = jnp.bfloat16
F32 = jnp.float32
NT = (((1,), (1,)), ((), ()))
TN = (((0,), (0,)), ((), ()))


MESH = pl.DeviceIdType.MESH
PART = 384
HALF = 1536


def place():
    dp = lax.axis_index("dp")
    sp = lax.axis_index("sp")
    return dp, sp, sp // 4, sp % 4


def sp_at(z, x):
    return (z + 4) % 4 * 4 + (x + 4) % 4


def dp_at(y, core):
    return (y + 4) % 4 * 2 + core


def greet():
    dp, sp, _, _ = place()
    barrier = pltpu.get_barrier_semaphore()
    for r in range(1, 16):
        pl.semaphore_signal(barrier, inc=1, device_id=(dp, (sp + r) % 16), device_id_type=MESH)
    for r in range(1, 8):
        pl.semaphore_signal(barrier, inc=1, device_id=((dp + r) % 8, sp), device_id_type=MESH)
    pl.semaphore_wait(barrier, 22)


def remote(src, dst, send, recv, dp, sp):
    return pltpu.make_async_remote_copy(
        src_ref=src, dst_ref=dst, send_sem=send, recv_sem=recv, device_id=(dp, sp), device_id_type=MESH
    )


class Sends:
    def __init__(self, sems):
        self.sems = sems
        self.started = []

    def go(self, src, dst, recv, dp, sp, when=None):
        copy = remote(src, dst, self.sems.at[len(self.started)], recv, dp, sp)
        self.started.append((copy, when))
        if when is None:
            copy.start()
        else:
            pl.when(when)(copy.start)

    def finish(self):
        for copy, when in self.started:
            if when is None:
                copy.wait_send()
            else:
                pl.when(when)(copy.wait_send)


def arrived(dst, recv):
    dp, sp, _, _ = place()
    remote(dst, dst, recv, recv, dp, sp).wait_recv()


SCALE = 1.0 / math.sqrt(SIZE)
FACTOR = SCALE * math.log2(math.e)
ANY = pl.BlockSpec(memory_space=pl.ANY)
DMA = pltpu.SemaphoreType.DMA


def lanes_of(i, width):
    return pl.ds(pl.multiple_of(i * width, width), width)


def forward_heads(c, qs, band, lb, bias, pb, rb, aa, an, dp):
    cols = lanes_of(c, SIZE)
    for h in range(2):
        head = 2 * c + h
        lanes = lanes_of(head, SIZE)
        q = qs[:, lanes]
        scores = []
        top = None
        for b in range(KB):
            k = band[0, b // 2, pl.ds(b % 2 * SIZE, SIZE), cols]
            s = lax.dot_general(k, q, NT, preferred_element_type=F32)
            s = s + bias[b * SIZE : (b + 1) * SIZE, :] + lb[head, b : b + 1, :]
            scores.append(s)
            t = jnp.max(s, axis=0, keepdims=True)
            top = t if top is None else jnp.maximum(top, t)
        total = jnp.zeros((1, TOK), F32)
        for b in range(KB):
            p = jnp.exp2((scores[b] - top) * FACTOR)
            total = total + jnp.sum(p, axis=0, keepdims=True)
            pb[head, b * SIZE : (b + 1) * SIZE, :] = p.astype(BF)
        v = band[1, :, :, cols].reshape(BAND, SIZE)
        out = lax.dot_general(v, pb[head], TN, preferred_element_type=F32)
        inverse = 1.0 / total
        rb[head] = jnp.broadcast_to(inverse, (8, TOK))
        out = out * inverse
        aa[dp, lanes, :] = out.astype(BF)
        an[:, lanes] = out.T.astype(BF)


def backward_heads(c, qs, band, pb, rb, aa, gt, dp):
    cols = lanes_of(c, SIZE)
    k = band[0, :, :, cols].reshape(BAND, SIZE)
    v = band[1, :, :, cols].reshape(BAND, SIZE)
    dk = jnp.zeros((BAND, SIZE), F32)
    dv = jnp.zeros((BAND, SIZE), F32)
    for h in range(2):
        head = 2 * c + h
        lanes = lanes_of(head, SIZE)
        inverse = rb[head, 0:1, :]
        g_t = gt[lanes, :].astype(F32)
        delta = jnp.sum(g_t * aa[dp, lanes, :].astype(F32), axis=0, keepdims=True) * inverse
        g_t = g_t * inverse
        g = g_t.T.astype(BF)
        grad_p = jnp.dot(v, g_t.astype(BF), preferred_element_type=F32)
        p = pb[head]
        grad_s = (p.astype(F32) * (grad_p - delta)).astype(BF)
        dq_t = lax.dot_general(k, grad_s, TN, preferred_element_type=F32)
        dk = dk + jnp.dot(grad_s, qs[:, lanes], preferred_element_type=F32)
        dv = dv + jnp.dot(p, g, preferred_element_type=F32)
        qs[:, lanes] = (dq_t * SCALE).T.astype(BF)
    band[0, :, :, cols] = (dk * SCALE).astype(BF).reshape(5, TOK, SIZE)
    band[1, :, :, cols] = dv.astype(BF).reshape(5, TOK, SIZE)


def layer_kernel(
    q_ref, k_ref, v_ref, list_ref, cnt_ref, len_ref, w_ref, d_ref,
    lo_ref, dq_ref, gkv_ref, gkv_z_ref, gb_ref,
    band, raw, lb, wb, db, qs, ds, bias, pb, rb, aa, an, gt, back, gw, rs, rx, gsum,
    local, kv_send, kv_recv, w_send, w_recv, pair_send, pair_recv, first_send, l_recv, d_recv,
    a_send, a_recv, row_send, row_recv, z_send, z_recv, rs_send, rs_recv, g_send, g_recv,
):
    dp, sp, z, x = place()
    y, core = dp // 2, dp % 2
    other = dp_at(y, 1 - core)
    loads = [
        pltpu.make_async_copy(k_ref, band.at[0, 4], local.at[0]),
        pltpu.make_async_copy(v_ref, band.at[1, 4], local.at[1]),
        pltpu.make_async_copy(w_ref.at[:, lanes_of(core, HALF)], wb.at[sp, :, lanes_of(core, HALF)], local.at[3]),
        pltpu.make_async_copy(d_ref.at[:, lanes_of(dp, PART)], db.at[dp], local.at[4]),
        pltpu.make_async_copy(q_ref, qs, local.at[5]),
        pltpu.make_async_copy(d_ref, ds, local.at[6]),
    ]
    for copy in loads:
        copy.start()
    greet()
    first_out = Sends(first_send)
    up, down = sp_at(z + 1, x), sp_at(z - 1, x)
    y_up, y_down, y_far = dp_at(y + 1, core), dp_at(y - 1, core), dp_at(y + 2, core)

    def kv_up(j):
        cols = lanes_of(j, 256)
        return remote(band.at[:, 4, :, cols], band.at[:, 0, :, cols], kv_send.at[0], kv_recv.at[0, j], dp, up)

    def kv_row(k, j):
        cols = lanes_of(j, 256)
        src = band.at[:, jnp.where(x + k < 4, 4, 0), :, cols]
        return remote(src, band.at[:, 4 - k, :, cols], kv_send.at[k], kv_recv.at[4 - k, j], dp, sp_at(z, x + k))

    def kv_rows(j, mine):
        for k in (2, 1, 3):
            pl.when((x + k < 4) if mine else (x + k >= 4))(kv_row(k, j).start)

    def kv_here(slot, j):
        arrived(band.at[:, slot, :, lanes_of(j, 256)], kv_recv.at[slot, j])

    half, other_half = lanes_of(core, HALF), lanes_of(1 - core, HALF)
    w_out = Sends(w_send)

    def weight(slot, first, rows, to):
        block = wb.at[slot, pl.ds(first, rows), half]
        w_out.go(block, block, w_recv.at[slot], dp, to)

    def weight_here(slot):
        arrived(wb.at[slot, :, half], w_recv.at[slot])

    def weight_z(slot):
        weight(slot, 0, 128, up)
        weight(slot, 0, 128, down)

    def weight_relay(dx, above):
        slot = sp_at(z + 1 if above else z - 1, x + dx)
        weight_here(slot)
        if above:
            weight(slot, 0, 96, down)
        else:
            weight(slot, 96, 32, up)

    def weight_pair(row):
        block = wb.at[pl.ds(4 * row, 4), :, half]
        remote(block, block, pair_send, pair_recv.at[row], other, sp).start()

    def grad_attn(row):
        arrived(wb.at[pl.ds(4 * row, 4), :, other_half], pair_recv.at[row])

        def one(i, _):
            i = 2 * row + i
            w = wb[pl.ds(2 * i, 2)].reshape(TOK, 3072)
            g = lax.dot_general(w, ds[...], NT, preferred_element_type=F32)
            gt[pl.ds(pl.multiple_of(i * TOK, TOK), TOK), :] = g.astype(BF)
            return 0

        lax.fori_loop(0, 2, one, 0)

    def spread(slot, j, first, rows, send, to):
        block = aa.at[slot, pl.ds(j * 512 + first, rows)]
        remote(block, block, send, a_recv.at[slot, j], to, sp).start()

    def spread_here(slot, j):
        arrived(aa.at[slot, pl.ds(j * 512, 512)], a_recv.at[slot, j])

    def spread_own(j):
        for i, to in enumerate((y_up, y_down, other)):
            spread(dp, j, 0, 512, a_send.at[i], to)

    def spread_on(j):
        spread_here(y_down, j)
        spread(y_down, j, 0, 256, a_send.at[3], y_up)
        spread(y_down, j, 0, 512, a_send.at[4], other)
        spread_here(y_up, j)
        spread(y_up, j, 256, 256, a_send.at[5], y_down)
        spread(y_up, j, 0, 512, a_send.at[6], other)

    def spread_far(j):
        spread_here(y_far, j)
        spread(y_far, j, 0, 512, a_send.at[7], other)

    diagonal = lax.broadcasted_iota(jnp.int32, (32, 32), 0) == lax.broadcasted_iota(jnp.int32, (32, 32), 1)
    used = jnp.max(jnp.where(diagonal, cnt_ref[...], 0), axis=1, keepdims=True)
    raw[sp] = jnp.full((32, 128), -100, jnp.int32)
    raw[sp, :, 0:8] = jnp.where(lax.broadcasted_iota(jnp.int32, (32, 8), 1) < used, list_ref[...], -100)

    for copy in loads[:3]:
        copy.wait()
    for dx in (1, 3, 2):
        weight(sp, 0, 128, sp_at(z, x + dx))
    kv_up(0).start()
    weight_z(sp)
    for j in (1, 2, 3):
        kv_up(j).start()
    for r in range(1, 16):
        first_out.go(raw.at[sp], raw.at[sp], l_recv, dp, (sp + r) % 16)
    for r in (2, 6, 4, 1, 3, 5, 7):
        to = (dp + r) % 8
        first_out.go(d_ref.at[:, lanes_of(to, PART)], db.at[dp], d_recv, to, sp)

    q_pos = sp * TOK + lax.broadcasted_iota(jnp.int32, (1, TOK), 1)
    begin = jnp.zeros((1, TOK), jnp.int32)
    start = jnp.int32(0)
    for i in range(16):
        begin = jnp.where(q_pos >= start, start, begin)
        start = start + len_ref[0, i]

    def mask(b, _):
        rows = pl.ds(pl.multiple_of(b * SIZE, SIZE), SIZE)
        k_pos = (sp - HALO) * TOK + b * SIZE + lax.broadcasted_iota(jnp.int32, (SIZE, TOK), 0)
        bias[rows, :] = jnp.where((k_pos <= q_pos) & (k_pos >= begin), 0.0, NEG)
        return 0

    lax.fori_loop(0, KB, mask, 0)

    for dx in (1, 3):
        weight_here(sp_at(z, x + dx))
        weight_z(sp_at(z, x + dx))
    kv_rows(0, True)
    kv_here(0, 0)
    kv_rows(0, False)
    kv_rows(1, True)
    weight_here(sp_at(z, x + 2))
    weight_z(sp_at(z, x + 2))
    weight_pair(z)
    for j in (1, 2):
        kv_here(0, j)
        kv_rows(j, False)
        kv_rows(j + 1, True)
    weight_relay(0, True)
    weight_relay(0, False)
    kv_here(0, 3)
    kv_rows(3, False)
    arrived(raw.at[pl.ds(0, 15)], l_recv)

    def list_terms(h, _):
        ids = 2 * sp - 2 * HALO + lax.broadcasted_iota(jnp.int32, (16, 128), 0)
        for i in range(2):
            found = jnp.where(raw[h, pl.ds(2 * sp + i, 1), :] == ids, 0.0, NEG)
            found = jnp.max(found, axis=1, keepdims=True)
            lb[h, :, i * SIZE : (i + 1) * SIZE] = jnp.broadcast_to(found, (16, SIZE))
        return 0

    lax.fori_loop(0, 16, list_terms, 0)
    for copy in loads[3:]:
        copy.wait()
    grad_attn(z)

    def forward(c, _):
        forward_heads(c, qs, band, lb, bias, pb, rb, aa, an, dp)
        return 0

    for j in range(4):
        for slot in (3, 1, 2):
            kv_here(slot, j)
        lax.fori_loop(2 * j, 2 * j + 2, forward, 0)
        spread_own(j)
        if j < 3:
            dx = (1, 3, 2)[j]
            weight_relay(dx, True)
            weight_relay(dx, False)
        if j > 0:
            spread_on(j - 1)
    row_above, row_below, row_far = (z + 1) % 4, (z + 3) % 4, (z + 2) % 4
    weight_pair(row_above)
    weight_pair(row_below)
    grad_attn(row_above)
    grad_attn(row_below)
    spread_on(3)
    for i in range(4):
        weight_here(4 * row_far + i)
    weight_pair(row_far)
    for j in range(3):
        spread_far(j)
    grad_attn(row_far)
    for k in range(4):
        remote(band.at[:, 0], band.at[:, 0], kv_send.at[k], kv_send.at[k], dp, up).wait_send()

    def backward(c, _):
        backward_heads(c, qs, band, pb, rb, aa, gt, dp)
        cols = lanes_of(c, SIZE)
        for k in (2, 1, 3):
            remote(
                band.at[:, 4 - k, :, cols], back.at[k - 1, :, :, cols], row_send.at[k - 1], row_recv.at[k - 1, c], dp, sp_at(z, x - k)
            ).start()
        return 0

    lax.fori_loop(0, 8, backward, 0)
    dq_out = pltpu.make_async_copy(qs, dq_ref, local.at[7])
    dq_out.start()
    spread_far(3)
    for r in range(4):
        for j in range(4):
            spread_here(dp_at(y + r, 1 - core), j)
    arrived(db.at[pl.ds(0, 7)], d_recv)

    def weight_grad(t, _):
        j = (z + 1 + t) % 4
        rows = pl.ds(pl.multiple_of(j * 512, 512), 512)
        total = jnp.zeros((512, PART), F32)
        for e in range(8):
            total = total + jnp.dot(aa[e, rows, :], db[e], preferred_element_type=F32)
        gw[pl.ds(4 * j, 4)] = total.astype(BF).reshape(4, 128, PART)

        @pl.when(t < 3)
        def _():
            remote(gw.at[pl.ds(4 * j, 4)], rs.at[pl.ds(4 * t, 4)], rs_send.at[0], rs_recv.at[0], dp, sp_at(j, x)).start()

        return 0

    lax.fori_loop(0, 4, weight_grad, 0)

    keep = [jnp.where(x + k < 4, 1.0, 0.0).astype(F32) for k in (1, 2, 3)]

    def z_copy(c):
        cols = lanes_of(c, SIZE)
        return remote(band.at[:, 0, :, cols], gkv_z_ref.at[:, :, cols], z_send, z_recv, dp, down)

    def row_sums(c, _):
        cols = lanes_of(c, SIZE)
        for k in range(3):
            arrived(back.at[k, :, :, cols], row_recv.at[k, c])
        below = band[:, 0, :, cols].astype(F32)
        here = band[:, 4, :, cols].astype(F32)
        for k in range(3):
            got = back[k, :, :, cols].astype(F32)
            here = here + got * keep[k]
            below = below + got * (1.0 - keep[k])
        band[:, 0, :, cols] = below.astype(BF)
        band[:, 4, :, cols] = here.astype(BF)
        z_copy(c).start()
        return 0


    def project(i, _):
        cols = lanes_of(i, 512)
        w = wb[:, :, cols].reshape(2048, 512)
        ds[:, cols] = jnp.dot(an[...], w, preferred_element_type=F32).astype(BF)
        return 0

    lax.fori_loop(0, 6, project, 0)
    lo_out = pltpu.make_async_copy(ds, lo_ref, local.at[8])
    lo_out.start()

    lax.fori_loop(0, 3, row_sums, 0)
    arrived(rs.at[pl.ds(0, 12)], rs_recv.at[0])

    def z_sums(i, _):
        total = gw[4 * z + i].astype(F32)
        for t in range(3):
            total = total + rs[4 * t + i].astype(F32)
        rs[12 + i] = total.astype(BF)

        @pl.when(i != x)
        def _():
            k = (x - i + 4) % 4 - 1
            remote(rs.at[12 + i], rx.at[k], rs_send.at[1], rs_recv.at[1], dp, sp_at(z, i)).start()

        return 0

    lax.fori_loop(0, 4, z_sums, 0)
    lax.fori_loop(3, 5, row_sums, 0)
    arrived(rx, rs_recv.at[1])
    total = rs[12 + x].astype(F32)
    for r in range(3):
        total = total + rx[r].astype(F32)
    gsum[...] = total.astype(BF)
    g_out = Sends(g_send)
    for r in range(1, 8):
        g_out.go(gsum, gb_ref.at[:, lanes_of(dp, PART)], g_recv, (dp + r) % 8, sp)
    own_sum = pltpu.make_async_copy(gsum, gb_ref.at[:, lanes_of(dp, PART)], local.at[9])
    own_sum.start()

    lax.fori_loop(5, 8, row_sums, 0)
    arrived(gkv_z_ref, z_recv)
    gkv_out = pltpu.make_async_copy(band.at[:, 4], gkv_ref, local.at[10])
    gkv_out.start()

    first_out.finish()
    w_out.finish()
    some = wb.at[:, :, half]
    remote(some, some, pair_send, pair_send, other, sp).wait_send()
    for i in range(8):
        some = aa.at[dp, pl.ds(0, 1024 if i in (3, 5) else 2048)]
        remote(some, some, a_send.at[i], a_send.at[i], other, sp).wait_send()
    for k in range(3):
        remote(back.at[k], back.at[k], row_send.at[k], row_send.at[k], dp, up).wait_send()
    remote(gkv_z_ref, gkv_z_ref, z_send, z_send, dp, down).wait_send()
    remote(rs.at[pl.ds(0, 12)], rs.at[pl.ds(0, 12)], rs_send.at[0], rs_send.at[0], dp, up).wait_send()
    remote(rx, rx, rs_send.at[1], rs_send.at[1], dp, up).wait_send()
    arrived(gb_ref.at[:, pl.ds(0, 7 * PART)], g_recv)
    g_out.finish()
    for copy in (dq_out, lo_out, own_sum, gkv_out):
        copy.wait()


def call_layer(q, k, v, lists, counts, lengths, w, d):
    vmem = pltpu.VMEM
    return pl.pallas_call(
        layer_kernel,
        in_specs=[ANY] * 3
        + [pl.BlockSpec(memory_space=vmem)] * 2
        + [pl.BlockSpec(memory_space=pltpu.SMEM)]
        + [ANY] * 2,
        out_specs=[ANY] * 5,
        out_shape=[
            jax.ShapeDtypeStruct((TOK, 3072), BF),
            jax.ShapeDtypeStruct((TOK, 2048), BF),
            jax.ShapeDtypeStruct((2, TOK, 1024), BF),
            jax.ShapeDtypeStruct((2, TOK, 1024), BF),
            jax.ShapeDtypeStruct((128, 3072), BF),
        ],
        scratch_shapes=[
            vmem((2, 5, TOK, 1024), BF),
            vmem((16, 32, 128), jnp.int32),
            vmem((16, 16, TOK), F32),
            vmem((16, 128, 3072), BF),
            vmem((8, TOK, PART), BF),
            vmem((TOK, 2048), BF),
            vmem((TOK, 3072), BF),
            vmem((BAND, TOK), F32),
            vmem((16, BAND, TOK), BF),
            vmem((16, 8, TOK), F32),
            vmem((8, 2048, TOK), BF),
            vmem((TOK, 2048), BF),
            vmem((2048, TOK), BF),
            vmem((3, 2, TOK, 1024), BF),
            vmem((16, 128, PART), BF),
            vmem((16, 128, PART), BF),
            vmem((3, 128, PART), BF),
            vmem((128, PART), BF),
            DMA((11,)),
            DMA((4,)),
            DMA((4, 4)),
            DMA((19,)),
            DMA((16,)),
            DMA,
            DMA((4,)),
            DMA((22,)),
            DMA,
            DMA,
            DMA((8,)),
            DMA((8, 4)),
            DMA((3,)),
            DMA((3, 8)),
            DMA,
            DMA,
            DMA((2,)),
            DMA((2,)),
            DMA((7,)),
            DMA,
        ],
        compiler_params=pltpu.CompilerParams(collective_id=0, has_side_effects=True, vmem_limit_bytes=60 * 2**20),
        cost_estimate=pl.CostEstimate(flops=27 * 10**9, bytes_accessed=20 * 10**6, transcendentals=6 * 10**6),
    )(q, k, v, lists, counts, lengths, w, d)


def per_device(queries, keys, values, key_blocks, block_counts, doc_lengths, out_weight, d_out):
    layer_out, grad_q, grad_kv, more_kv, grad_all = call_layer(
        queries[0], keys[0], values[0], key_blocks[0, 0], block_counts[0], doc_lengths, out_weight, d_out[0]
    )
    grad_kv = (grad_kv.astype(F32) + more_kv.astype(F32)).astype(BF)
    grad_weight = grad_all.astype(F32)
    tokens = lax.axis_size("dp") * lax.axis_size("sp") * TOK
    grad_weight = grad_weight * (1.0 / math.sqrt(tokens))
    return (layer_out[None], grad_q[None], grad_kv[:1], grad_kv[1:], grad_weight)


def solution(mesh):
    in_specs = (
        P("dp", "sp", None),
        P("dp", "sp", None),
        P("dp", "sp", None),
        P("dp", "sp", None, None),
        P("dp", "sp", None),
        P("dp", None),
        P("sp", None),
        P("dp", "sp", None),
    )
    out_specs = (
        P("dp", "sp", None),
        P("dp", "sp", None),
        P("dp", "sp", None),
        P("dp", "sp", None),
        P("sp", None),
    )
    return jax.shard_map(per_device, mesh=mesh, in_specs=in_specs, out_specs=out_specs, check_vma=False)
```

```python
import math

import jax
import jax.numpy as jnp
from jax import lax
from jax.experimental import pallas as pl
from jax.experimental.pallas import tpu as pltpu
from jax.sharding import PartitionSpec as P

SIZE = 128
TOK = 256
HALO = 4
BAND = (HALO + 1) * TOK
KB = BAND // SIZE
NEG = -1e30
BF = jnp.bfloat16
F32 = jnp.float32
NT = (((1,), (1,)), ((), ()))
TN = (((0,), (0,)), ((), ()))


MESH = pl.DeviceIdType.MESH
PART = 384
HALF = 1536


def place():
    dp = lax.axis_index("dp")
    sp = lax.axis_index("sp")
    return dp, sp, sp // 4, sp % 4


def sp_at(z, x):
    return (z + 4) % 4 * 4 + (x + 4) % 4


def dp_at(y, core):
    return (y + 4) % 4 * 2 + core


def greet():
    dp, sp, _, _ = place()
    barrier = pltpu.get_barrier_semaphore()
    for r in range(1, 16):
        pl.semaphore_signal(barrier, inc=1, device_id=(dp, (sp + r) % 16), device_id_type=MESH)
    for r in range(1, 8):
        pl.semaphore_signal(barrier, inc=1, device_id=((dp + r) % 8, sp), device_id_type=MESH)
    pl.semaphore_wait(barrier, 22)


def remote(src, dst, send, recv, dp, sp):
    return pltpu.make_async_remote_copy(
        src_ref=src, dst_ref=dst, send_sem=send, recv_sem=recv, device_id=(dp, sp), device_id_type=MESH
    )


class Sends:
    def __init__(self, sems):
        self.sems = sems
        self.started = []

    def go(self, src, dst, recv, dp, sp, when=None):
        copy = remote(src, dst, self.sems.at[len(self.started)], recv, dp, sp)
        self.started.append((copy, when))
        if when is None:
            copy.start()
        else:
            pl.when(when)(copy.start)

    def finish(self):
        for copy, when in self.started:
            if when is None:
                copy.wait_send()
            else:
                pl.when(when)(copy.wait_send)


def arrived(dst, recv):
    dp, sp, _, _ = place()
    remote(dst, dst, recv, recv, dp, sp).wait_recv()


SCALE = 1.0 / math.sqrt(SIZE)
FACTOR = SCALE * math.log2(math.e)
ANY = pl.BlockSpec(memory_space=pl.ANY)
DMA = pltpu.SemaphoreType.DMA


def lanes_of(i, width):
    return pl.ds(pl.multiple_of(i * width, width), width)


def forward_heads(c, qs, band, lb, bias, pb, rb, aa, an, dp):
    cols = lanes_of(c, SIZE)
    for h in range(2):
        head = 2 * c + h
        lanes = lanes_of(head, SIZE)
        q = qs[:, lanes]
        scores = []
        top = None
        for b in range(KB):
            k = band[0, b // 2, pl.ds(b % 2 * SIZE, SIZE), cols]
            s = lax.dot_general(k, q, NT, preferred_element_type=F32)
            s = s + bias[b * SIZE : (b + 1) * SIZE, :] + lb[head, b : b + 1, :]
            scores.append(s)
            t = jnp.max(s, axis=0, keepdims=True)
            top = t if top is None else jnp.maximum(top, t)
        total = jnp.zeros((1, TOK), F32)
        for b in range(KB):
            p = jnp.exp2((scores[b] - top) * FACTOR)
            total = total + jnp.sum(p, axis=0, keepdims=True)
            pb[head, b * SIZE : (b + 1) * SIZE, :] = p.astype(BF)
        v = band[1, :, :, cols].reshape(BAND, SIZE)
        out = lax.dot_general(v, pb[head], TN, preferred_element_type=F32)
        inverse = 1.0 / total
        rb[head] = jnp.broadcast_to(inverse, (8, TOK))
        out = out * inverse
        aa[dp, lanes, :] = out.astype(BF)
        an[:, lanes] = out.T.astype(BF)


def backward_heads(c, qs, band, pb, rb, aa, gt, dp):
    cols = lanes_of(c, SIZE)
    k = band[0, :, :, cols].reshape(BAND, SIZE)
    v = band[1, :, :, cols].reshape(BAND, SIZE)
    dk = jnp.zeros((BAND, SIZE), F32)
    dv = jnp.zeros((BAND, SIZE), F32)
    for h in range(2):
        head = 2 * c + h
        lanes = lanes_of(head, SIZE)
        inverse = rb[head, 0:1, :]
        g_t = gt[lanes, :].astype(F32)
        delta = jnp.sum(g_t * aa[dp, lanes, :].astype(F32), axis=0, keepdims=True) * inverse
        g_t = g_t * inverse
        g = g_t.T.astype(BF)
        grad_p = jnp.dot(v, g_t.astype(BF), preferred_element_type=F32)
        p = pb[head]
        grad_s = (p.astype(F32) * (grad_p - delta)).astype(BF)
        dq_t = lax.dot_general(k, grad_s, TN, preferred_element_type=F32)
        dk = dk + jnp.dot(grad_s, qs[:, lanes], preferred_element_type=F32)
        dv = dv + jnp.dot(p, g, preferred_element_type=F32)
        qs[:, lanes] = (dq_t * SCALE).T.astype(BF)
    band[0, :, :, cols] = (dk * SCALE).astype(BF).reshape(5, TOK, SIZE)
    band[1, :, :, cols] = dv.astype(BF).reshape(5, TOK, SIZE)


def layer_kernel(
    q_ref, k_ref, v_ref, list_ref, cnt_ref, len_ref, w_ref, d_ref,
    lo_ref, dq_ref, gkv_ref, gkv_z_ref, gb_ref,
    band, raw, lb, wb, db, qs, ds, bias, pb, rb, aa, an, gt, back, gw, rs, rx, gsum,
    local, kv_send, kv_recv, w_send, w_recv, q_recv, pair_send, pair_recv, first_send, l_recv, d_recv,
    a_send, a_recv, row_send, row_recv, z_send, z_recv, rs_send, rs_recv, g_send, g_recv,
):
    dp, sp, z, x = place()
    y, core = dp // 2, dp % 2
    other = dp_at(y, 1 - core)
    loads = [
        pltpu.make_async_copy(k_ref, band.at[0, 4], local.at[0]),
        pltpu.make_async_copy(v_ref, band.at[1, 4], local.at[1]),
        pltpu.make_async_copy(w_ref.at[:, lanes_of(core, HALF)], wb.at[sp, :, lanes_of(core, HALF)], local.at[3]),
        pltpu.make_async_copy(d_ref.at[:, lanes_of(dp, PART)], db.at[dp], local.at[4]),
        pltpu.make_async_copy(q_ref, qs, local.at[5]),
        pltpu.make_async_copy(d_ref, ds, local.at[6]),
    ]
    for copy in loads:
        copy.start()
    greet()
    def chunks(row):
        return [(row + i) % 4 for i in (0, 1, 3, 2)]

    order = chunks(z)
    first_out = Sends(first_send)
    up, down = sp_at(z + 1, x), sp_at(z - 1, x)
    y_up, y_down, y_far = dp_at(y + 1, core), dp_at(y - 1, core), dp_at(y + 2, core)

    def kv_up(j):
        cols = lanes_of(j, 256)
        return remote(band.at[:, 4, :, cols], band.at[:, 0, :, cols], kv_send.at[0, j], kv_recv.at[0, j], dp, up)

    def kv_row(k, j):
        cols = lanes_of(j, 256)
        src = band.at[:, jnp.where(x + k < 4, 4, 0), :, cols]
        return remote(src, band.at[:, 4 - k, :, cols], kv_send.at[k, j], kv_recv.at[4 - k, j], dp, sp_at(z, x + k))

    def kv_rows(j, mine):
        for k in (2, 1, 3):
            pl.when((x + k < 4) if mine else (x + k >= 4))(kv_row(k, j).start)

    def kv_here(slot, j):
        arrived(band.at[:, slot, :, lanes_of(j, 256)], kv_recv.at[slot, j])

    half, other_half = lanes_of(core, HALF), lanes_of(1 - core, HALF)
    w_out = Sends(w_send)

    def weight(slot, first, rows, to):
        block = wb.at[slot, pl.ds(first, rows), half]
        w_out.go(block, block, w_recv.at[slot], dp, to)

    def weight_here(slot):
        arrived(wb.at[slot, :, half], w_recv.at[slot])

    def weight_quarter(slot, recv, to_dp, to_sp):
        block = wb.at[slot, pl.ds(pl.multiple_of(32 * y, 32), 32), half]
        w_out.go(block, block, recv, to_dp, to_sp)

    def weight_quarter_here(slot):
        arrived(wb.at[slot, pl.ds(0, 32), half], q_recv.at[slot])
        for dy in (1, 3, 2):
            weight_quarter(slot, w_recv.at[slot], dp_at(y + dy, core), sp)

    def weight_rest_here(slot):
        arrived(wb.at[slot, pl.ds(0, 96), half], w_recv.at[slot])

    def weight_z(slot):
        weight(slot, 0, 128, up)
        weight(slot, 0, 128, down)

    def weight_relay(dx, above):
        slot = sp_at(z + 1 if above else z - 1, x + dx)
        weight_here(slot)
        if above:
            weight(slot, 0, 96, down)
        else:
            weight(slot, 96, 32, up)

    def weight_pair(row):
        block = wb.at[pl.ds(4 * row, 4), :, half]
        remote(block, block, pair_send, pair_recv.at[row], other, sp).start()

    def grad_attn(row):
        arrived(wb.at[pl.ds(4 * row, 4), :, other_half], pair_recv.at[row])

        def one(i, _):
            i = 2 * row + i
            w = wb[pl.ds(2 * i, 2)].reshape(TOK, 3072)
            g = lax.dot_general(w, ds[...], NT, preferred_element_type=F32)
            gt[pl.ds(pl.multiple_of(i * TOK, TOK), TOK), :] = g.astype(BF)
            return 0

        lax.fori_loop(0, 2, one, 0)

    def spread(slot, j, first, rows, send, to):
        block = aa.at[slot, pl.ds(j * 512 + first, rows)]
        remote(block, block, send, a_recv.at[slot, j], to, sp).start()

    def spread_here(slot, j):
        arrived(aa.at[slot, pl.ds(j * 512, 512)], a_recv.at[slot, j])

    def spread_own(j):
        for i, to in enumerate((y_up, y_down, other)):
            spread(dp, j, 0, 512, a_send.at[i], to)

    def spread_on(j):
        spread_here(y_down, j)
        spread(y_down, j, 0, 256, a_send.at[3], y_up)
        spread(y_down, j, 0, 512, a_send.at[4], other)
        spread_here(y_up, j)
        spread(y_up, j, 256, 256, a_send.at[5], y_down)
        spread(y_up, j, 0, 512, a_send.at[6], other)

    def spread_far(j):
        spread_here(y_far, j)
        spread(y_far, j, 0, 512, a_send.at[7], other)

    diagonal = lax.broadcasted_iota(jnp.int32, (32, 32), 0) == lax.broadcasted_iota(jnp.int32, (32, 32), 1)
    used = jnp.max(jnp.where(diagonal, cnt_ref[...], 0), axis=1, keepdims=True)
    raw[sp] = jnp.full((32, 128), -100, jnp.int32)
    raw[sp, :, 0:8] = jnp.where(lax.broadcasted_iota(jnp.int32, (32, 8), 1) < used, list_ref[...], -100)

    for copy in loads[:3]:
        copy.wait()
    for dx in (1, 3, 2):
        weight_quarter(sp, q_recv.at[sp], dp, sp_at(z, x + dx))
    first, *others = chunks(z + 1)
    kv_up(first).start()
    weight_z(sp)
    for j in others:
        kv_up(j).start()
    for r in range(1, 16):
        first_out.go(raw.at[sp], raw.at[sp], l_recv, dp, (sp + r) % 16)

    q_pos = sp * TOK + lax.broadcasted_iota(jnp.int32, (1, TOK), 1)
    begin = jnp.zeros((1, TOK), jnp.int32)
    start = jnp.int32(0)
    for i in range(16):
        begin = jnp.where(q_pos >= start, start, begin)
        start = start + len_ref[0, i]

    def mask(b, _):
        rows = pl.ds(pl.multiple_of(b * SIZE, SIZE), SIZE)
        k_pos = (sp - HALO) * TOK + b * SIZE + lax.broadcasted_iota(jnp.int32, (SIZE, TOK), 0)
        bias[rows, :] = jnp.where((k_pos <= q_pos) & (k_pos >= begin), 0.0, NEG)
        return 0

    lax.fori_loop(0, KB, mask, 0)

    for dx in (1, 3, 2):
        weight_quarter_here(sp_at(z, x + dx))
    kv_rows(order[0], True)
    kv_rows(order[1], True)
    kv_here(0, order[0])
    kv_rows(order[0], False)
    for dx in (1, 3, 2):
        weight_rest_here(sp_at(z, x + dx))
        weight_z(sp_at(z, x + dx))
    weight_pair(z)
    for r in (2, 6, 4, 1, 3, 5, 7):
        to = (dp + r) % 8
        first_out.go(d_ref.at[:, lanes_of(to, PART)], db.at[dp], d_recv, to, sp)
    kv_here(0, order[1])
    kv_rows(order[1], False)
    kv_rows(order[2], True)
    arrived(raw.at[pl.ds(0, 15)], l_recv)

    def list_terms(h, _):
        ids = 2 * sp - 2 * HALO + lax.broadcasted_iota(jnp.int32, (16, 128), 0)
        for i in range(2):
            found = jnp.where(raw[h, pl.ds(2 * sp + i, 1), :] == ids, 0.0, NEG)
            found = jnp.max(found, axis=1, keepdims=True)
            lb[h, :, i * SIZE : (i + 1) * SIZE] = jnp.broadcast_to(found, (16, SIZE))
        return 0

    lax.fori_loop(0, 16, list_terms, 0)
    for copy in loads[3:]:
        copy.wait()
    kv_here(0, order[2])
    kv_rows(order[2], False)
    kv_rows(order[3], True)
    grad_attn(z)

    def forward(c, _):
        forward_heads(c, qs, band, lb, bias, pb, rb, aa, an, dp)
        return 0

    def backward(c, _):
        backward_heads(c, qs, band, pb, rb, aa, gt, dp)
        return 0

    def backward_chunk(j):
        cols = lanes_of(j, 256)
        for k in range(4):
            remote(band.at[:, 0, :, cols], band.at[:, 0, :, cols], kv_send.at[k, j], kv_send.at[k, j], dp, up).wait_send()
        lax.fori_loop(2 * j, 2 * j + 2, backward, 0)

    def give_back(j):
        cols = lanes_of(j, 256)
        for k in (2, 1, 3):
            remote(
                band.at[:, 4 - k, :, cols], back.at[k - 1, :, :, cols], row_send.at[k - 1], row_recv.at[k - 1, j], dp, sp_at(z, x - k)
            ).start()

    def spread_in(j):
        for r in range(4):
            spread_here(dp_at(y + r, 1 - core), j)

    def weight_grad(j):
        rows = pl.ds(pl.multiple_of(j * 512, 512), 512)
        total = jnp.zeros((512, PART), F32)
        for e in range(8):
            total = total + jnp.dot(aa[e, rows, :], db[e], preferred_element_type=F32)
        gw[pl.ds(4 * j, 4)] = total.astype(BF).reshape(4, 128, PART)

    def scatter_z(j):
        k = (z - j + 4) % 4 - 1
        remote(gw.at[pl.ds(4 * j, 4)], rs.at[pl.ds(4 * k, 4)], rs_send.at[0], rs_recv.at[0], dp, sp_at(j, x)).start()

    def kv_chunk(j):
        for slot in (3, 1, 2):
            kv_here(slot, j)

    def forward_chunk(j):
        lax.fori_loop(2 * j, 2 * j + 2, forward, 0)
        spread_own(j)

    own_row, row_above, row_below, row_far = order

    kv_chunk(own_row)
    forward_chunk(own_row)
    kv_here(0, order[3])
    kv_rows(order[3], False)
    weight_relay(0, True)
    weight_relay(1, True)
    weight_relay(0, False)
    weight_relay(1, False)
    backward_chunk(own_row)
    weight_relay(3, True)
    weight_relay(3, False)
    spread_on(own_row)

    kv_chunk(row_above)
    forward_chunk(row_above)
    weight_relay(2, True)
    weight_pair(row_above)
    weight_relay(2, False)
    weight_pair(row_below)
    grad_attn(row_above)
    backward_chunk(row_above)
    spread_on(row_above)
    spread_far(own_row)

    kv_chunk(row_below)
    give_back(own_row)
    forward_chunk(row_below)
    grad_attn(row_below)
    backward_chunk(row_below)
    spread_on(row_below)
    spread_far(row_above)
    arrived(db.at[pl.ds(0, 7)], d_recv)
    spread_in(own_row)
    weight_grad(own_row)
    for i in range(4):
        weight_here(4 * row_far + i)
    weight_pair(row_far)

    kv_chunk(row_far)
    give_back(row_above)
    give_back(row_below)
    forward_chunk(row_far)
    grad_attn(row_far)
    backward_chunk(row_far)
    give_back(row_far)
    dq_out = pltpu.make_async_copy(qs, dq_ref, local.at[7])
    dq_out.start()
    spread_on(row_far)
    spread_far(row_below)
    spread_in(row_above)
    weight_grad(row_above)
    scatter_z(row_above)
    spread_far(row_far)
    spread_in(row_below)
    weight_grad(row_below)
    scatter_z(row_below)
    spread_in(row_far)
    weight_grad(row_far)
    scatter_z(row_far)
    keep = [jnp.where(x + k < 4, 1.0, 0.0).astype(F32) for k in (1, 2, 3)]

    def z_copy(j):
        cols = lanes_of(j, 256)
        return remote(band.at[:, 0, :, cols], gkv_z_ref.at[:, :, cols], z_send, z_recv, dp, down)

    def row_sums(j):
        for k in range(3):
            arrived(back.at[k, :, :, lanes_of(j, 256)], row_recv.at[k, j])

        def one(c, _):
            cols = lanes_of(c, SIZE)
            below = band[:, 0, :, cols].astype(F32)
            here = band[:, 4, :, cols].astype(F32)
            for k in range(3):
                got = back[k, :, :, cols].astype(F32)
                here = here + got * keep[k]
                below = below + got * (1.0 - keep[k])
            band[:, 0, :, cols] = below.astype(BF)
            band[:, 4, :, cols] = here.astype(BF)
            return 0

        lax.fori_loop(2 * j, 2 * j + 2, one, 0)
        z_copy(j).start()

    def project(i, _):
        cols = lanes_of(i, 512)
        w = wb[:, :, cols].reshape(2048, 512)
        ds[:, cols] = jnp.dot(an[...], w, preferred_element_type=F32).astype(BF)
        return 0

    lax.fori_loop(0, 6, project, 0)
    lo_out = pltpu.make_async_copy(ds, lo_ref, local.at[8])
    lo_out.start()

    row_sums(own_row)
    arrived(rs.at[pl.ds(0, 12)], rs_recv.at[0])

    def z_sums(i, _):
        total = gw[4 * z + i].astype(F32)
        for t in range(3):
            total = total + rs[4 * t + i].astype(F32)
        rs[12 + i] = total.astype(BF)

        @pl.when(i != x)
        def _():
            k = (x - i + 4) % 4 - 1
            remote(rs.at[12 + i], rx.at[k], rs_send.at[1], rs_recv.at[1], dp, sp_at(z, i)).start()

        return 0

    lax.fori_loop(0, 4, z_sums, 0)
    row_sums(row_above)
    arrived(rx, rs_recv.at[1])
    total = rs[12 + x].astype(F32)
    for r in range(3):
        total = total + rx[r].astype(F32)
    gsum[...] = total.astype(BF)
    g_out = Sends(g_send)
    for r in range(1, 8):
        g_out.go(gsum, gb_ref.at[:, lanes_of(dp, PART)], g_recv, (dp + r) % 8, sp)
    own_sum = pltpu.make_async_copy(gsum, gb_ref.at[:, lanes_of(dp, PART)], local.at[9])
    own_sum.start()

    row_sums(row_below)
    row_sums(row_far)
    arrived(gkv_z_ref, z_recv)
    gkv_out = pltpu.make_async_copy(band.at[:, 4], gkv_ref, local.at[10])
    gkv_out.start()

    first_out.finish()
    w_out.finish()
    some = wb.at[:, :, half]
    remote(some, some, pair_send, pair_send, other, sp).wait_send()
    for i in range(8):
        some = aa.at[dp, pl.ds(0, 1024 if i in (3, 5) else 2048)]
        remote(some, some, a_send.at[i], a_send.at[i], other, sp).wait_send()
    for k in range(3):
        remote(back.at[k], back.at[k], row_send.at[k], row_send.at[k], dp, up).wait_send()
    remote(gkv_z_ref, gkv_z_ref, z_send, z_send, dp, down).wait_send()
    remote(rs.at[pl.ds(0, 12)], rs.at[pl.ds(0, 12)], rs_send.at[0], rs_send.at[0], dp, up).wait_send()
    remote(rx, rx, rs_send.at[1], rs_send.at[1], dp, up).wait_send()
    arrived(gb_ref.at[:, pl.ds(0, 7 * PART)], g_recv)
    g_out.finish()
    for copy in (dq_out, lo_out, own_sum, gkv_out):
        copy.wait()


def call_layer(q, k, v, lists, counts, lengths, w, d):
    vmem = pltpu.VMEM
    return pl.pallas_call(
        layer_kernel,
        in_specs=[ANY] * 3
        + [pl.BlockSpec(memory_space=vmem)] * 2
        + [pl.BlockSpec(memory_space=pltpu.SMEM)]
        + [ANY] * 2,
        out_specs=[ANY] * 5,
        out_shape=[
            jax.ShapeDtypeStruct((TOK, 3072), BF),
            jax.ShapeDtypeStruct((TOK, 2048), BF),
            jax.ShapeDtypeStruct((2, TOK, 1024), BF),
            jax.ShapeDtypeStruct((2, TOK, 1024), BF),
            jax.ShapeDtypeStruct((128, 3072), BF),
        ],
        scratch_shapes=[
            vmem((2, 5, TOK, 1024), BF),
            vmem((16, 32, 128), jnp.int32),
            vmem((16, 16, TOK), F32),
            vmem((16, 128, 3072), BF),
            vmem((8, TOK, PART), BF),
            vmem((TOK, 2048), BF),
            vmem((TOK, 3072), BF),
            vmem((BAND, TOK), F32),
            vmem((16, BAND, TOK), BF),
            vmem((16, 8, TOK), F32),
            vmem((8, 2048, TOK), BF),
            vmem((TOK, 2048), BF),
            vmem((2048, TOK), BF),
            vmem((3, 2, TOK, 1024), BF),
            vmem((16, 128, PART), BF),
            vmem((16, 128, PART), BF),
            vmem((3, 128, PART), BF),
            vmem((128, PART), BF),
            DMA((11,)),
            DMA((4, 4)),
            DMA((4, 4)),
            DMA((28,)),
            DMA((16,)),
            DMA((16,)),
            DMA,
            DMA((4,)),
            DMA((22,)),
            DMA,
            DMA,
            DMA((8,)),
            DMA((8, 4)),
            DMA((3,)),
            DMA((3, 4)),
            DMA,
            DMA,
            DMA((2,)),
            DMA((2,)),
            DMA((7,)),
            DMA,
        ],
        compiler_params=pltpu.CompilerParams(collective_id=0, has_side_effects=True, vmem_limit_bytes=60 * 2**20),
        cost_estimate=pl.CostEstimate(flops=27 * 10**9, bytes_accessed=20 * 10**6, transcendentals=6 * 10**6),
    )(q, k, v, lists, counts, lengths, w, d)


def per_device(queries, keys, values, key_blocks, block_counts, doc_lengths, out_weight, d_out):
    layer_out, grad_q, grad_kv, more_kv, grad_all = call_layer(
        queries[0], keys[0], values[0], key_blocks[0, 0], block_counts[0], doc_lengths, out_weight, d_out[0]
    )
    grad_kv = (grad_kv.astype(F32) + more_kv.astype(F32)).astype(BF)
    grad_weight = grad_all.astype(F32)
    tokens = lax.axis_size("dp") * lax.axis_size("sp") * TOK
    grad_weight = grad_weight * (1.0 / math.sqrt(tokens))
    return (layer_out[None], grad_q[None], grad_kv[:1], grad_kv[1:], grad_weight)


def solution(mesh):
    in_specs = (
        P("dp", "sp", None),
        P("dp", "sp", None),
        P("dp", "sp", None),
        P("dp", "sp", None, None),
        P("dp", "sp", None),
        P("dp", None),
        P("sp", None),
        P("dp", "sp", None),
    )
    out_specs = (
        P("dp", "sp", None),
        P("dp", "sp", None),
        P("dp", "sp", None),
        P("dp", "sp", None),
        P("sp", None),
    )
    return jax.shard_map(per_device, mesh=mesh, in_specs=in_specs, out_specs=out_specs, check_vma=False)
```

```python
import math

import jax
import jax.numpy as jnp
from jax import lax
from jax.experimental import pallas as pl
from jax.experimental.pallas import tpu as pltpu
from jax.sharding import PartitionSpec as P

SIZE = 128
TOK = 256
HALO = 4
BAND = (HALO + 1) * TOK
KB = BAND // SIZE
NEG = -1e30
BF = jnp.bfloat16
F32 = jnp.float32
NT = (((1,), (1,)), ((), ()))
TN = (((0,), (0,)), ((), ()))


MESH = pl.DeviceIdType.MESH
PART = 384
HALF = 1536


def place():
    dp = lax.axis_index("dp")
    sp = lax.axis_index("sp")
    return dp, sp, sp // 4, sp % 4


def sp_at(z, x):
    return (z + 4) % 4 * 4 + (x + 4) % 4


def dp_at(y, core):
    return (y + 4) % 4 * 2 + core


def greet():
    dp, sp, _, _ = place()
    barrier = pltpu.get_barrier_semaphore()
    for r in range(1, 16):
        pl.semaphore_signal(barrier, inc=1, device_id=(dp, (sp + r) % 16), device_id_type=MESH)
    for r in range(1, 8):
        pl.semaphore_signal(barrier, inc=1, device_id=((dp + r) % 8, sp), device_id_type=MESH)
    pl.semaphore_wait(barrier, 22)


def remote(src, dst, send, recv, dp, sp):
    return pltpu.make_async_remote_copy(
        src_ref=src, dst_ref=dst, send_sem=send, recv_sem=recv, device_id=(dp, sp), device_id_type=MESH
    )


class Sends:
    def __init__(self, sems):
        self.sems = sems
        self.started = []

    def go(self, src, dst, recv, dp, sp, when=None):
        copy = remote(src, dst, self.sems.at[len(self.started)], recv, dp, sp)
        self.started.append((copy, when))
        if when is None:
            copy.start()
        else:
            pl.when(when)(copy.start)

    def finish(self):
        for copy, when in self.started:
            if when is None:
                copy.wait_send()
            else:
                pl.when(when)(copy.wait_send)


def arrived(dst, recv):
    dp, sp, _, _ = place()
    remote(dst, dst, recv, recv, dp, sp).wait_recv()


SCALE = 1.0 / math.sqrt(SIZE)
FACTOR = SCALE * math.log2(math.e)
ANY = pl.BlockSpec(memory_space=pl.ANY)
DMA = pltpu.SemaphoreType.DMA


def lanes_of(i, width):
    return pl.ds(pl.multiple_of(i * width, width), width)


def forward_heads(c, qs, band, lb, bias, pb, rb, aa, an, dp):
    cols = lanes_of(c, SIZE)
    for h in range(2):
        head = 2 * c + h
        lanes = lanes_of(head, SIZE)
        q = qs[:, lanes]
        scores = []
        top = None
        for b in range(KB):
            k = band[0, b // 2, pl.ds(b % 2 * SIZE, SIZE), cols]
            s = lax.dot_general(k, q, NT, preferred_element_type=F32)
            s = s + bias[b * SIZE : (b + 1) * SIZE, :] + lb[head, b : b + 1, :]
            scores.append(s)
            t = jnp.max(s, axis=0, keepdims=True)
            top = t if top is None else jnp.maximum(top, t)
        total = jnp.zeros((1, TOK), F32)
        for b in range(KB):
            p = jnp.exp2((scores[b] - top) * FACTOR)
            total = total + jnp.sum(p, axis=0, keepdims=True)
            pb[head, b * SIZE : (b + 1) * SIZE, :] = p.astype(BF)
        v = band[1, :, :, cols].reshape(BAND, SIZE)
        out = lax.dot_general(v, pb[head], TN, preferred_element_type=F32)
        inverse = 1.0 / total
        rb[head] = jnp.broadcast_to(inverse, (8, TOK))
        out = out * inverse
        aa[dp, lanes, :] = out.astype(BF)
        an[:, lanes] = out.T.astype(BF)


def backward_heads(c, qs, band, pb, rb, aa, gt, dp):
    cols = lanes_of(c, SIZE)
    k = band[0, :, :, cols].reshape(BAND, SIZE)
    v = band[1, :, :, cols].reshape(BAND, SIZE)
    dk = jnp.zeros((BAND, SIZE), F32)
    dv = jnp.zeros((BAND, SIZE), F32)
    for h in range(2):
        head = 2 * c + h
        lanes = lanes_of(head, SIZE)
        inverse = rb[head, 0:1, :]
        g_t = gt[lanes, :].astype(F32)
        delta = jnp.sum(g_t * aa[dp, lanes, :].astype(F32), axis=0, keepdims=True) * inverse
        g_t = g_t * inverse
        g = g_t.T.astype(BF)
        grad_p = jnp.dot(v, g_t.astype(BF), preferred_element_type=F32)
        p = pb[head]
        grad_s = (p.astype(F32) * (grad_p - delta)).astype(BF)
        dq_t = lax.dot_general(k, grad_s, TN, preferred_element_type=F32)
        dk = dk + jnp.dot(grad_s, qs[:, lanes], preferred_element_type=F32)
        dv = dv + jnp.dot(p, g, preferred_element_type=F32)
        qs[:, lanes] = (dq_t * SCALE).T.astype(BF)
    band[0, :, :, cols] = (dk * SCALE).astype(BF).reshape(5, TOK, SIZE)
    band[1, :, :, cols] = dv.astype(BF).reshape(5, TOK, SIZE)


def layer_kernel(
    q_ref, k_ref, v_ref, list_ref, cnt_ref, len_ref, w_ref, d_ref,
    lo_ref, dq_ref, gk_ref, gv_ref, gk_z_ref, gv_z_ref, gb_ref,
    band, raw, lb, wb, db, qs, ds, bias, pb, rb, aa, an, gt, back, gw, rs, rx, gsum,
    local, kv_send, kv_recv, w_send, w_recv, q_recv, pair_send, pair_recv, first_send, l_recv, d_recv,
    a_send, a_recv, row_send, row_recv, z_send, z_recv, rs_send, rs_recv, g_send, g_recv,
):
    dp, sp, z, x = place()
    y, core = dp // 2, dp % 2
    other = dp_at(y, 1 - core)
    loads = [
        pltpu.make_async_copy(k_ref, band.at[0, 4], local.at[0]),
        pltpu.make_async_copy(v_ref, band.at[1, 4], local.at[1]),
        pltpu.make_async_copy(w_ref.at[:, lanes_of(core, HALF)], wb.at[sp, :, lanes_of(core, HALF)], local.at[3]),
        pltpu.make_async_copy(d_ref.at[:, lanes_of(dp, PART)], db.at[dp], local.at[4]),
        pltpu.make_async_copy(q_ref, qs, local.at[5]),
        pltpu.make_async_copy(d_ref, ds, local.at[6]),
    ]
    for copy in loads:
        copy.start()
    greet()
    def chunks(row):
        return [(row + i) % 4 for i in (0, 1, 3, 2)]

    order = chunks(z)
    first_out = Sends(first_send)
    up, down = sp_at(z + 1, x), sp_at(z - 1, x)
    y_up, y_down, y_far = dp_at(y + 1, core), dp_at(y - 1, core), dp_at(y + 2, core)

    def kv_up(j):
        cols = lanes_of(j, 256)
        return remote(band.at[:, 4, :, cols], band.at[:, 0, :, cols], kv_send.at[0, j], kv_recv.at[0, j], dp, up)

    def kv_row(k, j):
        cols = lanes_of(j, 256)
        src = band.at[:, jnp.where(x + k < 4, 4, 0), :, cols]
        return remote(src, band.at[:, 4 - k, :, cols], kv_send.at[k, j], kv_recv.at[4 - k, j], dp, sp_at(z, x + k))

    def kv_rows(j, mine):
        for k in (2, 1, 3):
            pl.when((x + k < 4) if mine else (x + k >= 4))(kv_row(k, j).start)

    def kv_here(slot, j):
        arrived(band.at[:, slot, :, lanes_of(j, 256)], kv_recv.at[slot, j])

    half, other_half = lanes_of(core, HALF), lanes_of(1 - core, HALF)
    w_out = Sends(w_send)

    def weight(slot, first, rows, to):
        block = wb.at[slot, pl.ds(first, rows), half]
        w_out.go(block, block, w_recv.at[slot], dp, to)

    def weight_here(slot):
        arrived(wb.at[slot, :, half], w_recv.at[slot])

    def weight_quarter(slot, recv, to_dp, to_sp):
        block = wb.at[slot, pl.ds(pl.multiple_of(32 * y, 32), 32), half]
        w_out.go(block, block, recv, to_dp, to_sp)

    def weight_quarter_here(slot):
        arrived(wb.at[slot, pl.ds(0, 32), half], q_recv.at[slot])
        for dy in (1, 3, 2):
            weight_quarter(slot, w_recv.at[slot], dp_at(y + dy, core), sp)

    def weight_rest_here(slot):
        arrived(wb.at[slot, pl.ds(0, 96), half], w_recv.at[slot])

    def weight_z(slot):
        weight(slot, 0, 128, up)
        weight(slot, 0, 128, down)

    def weight_relay(dx, above):
        slot = sp_at(z + 1 if above else z - 1, x + dx)
        weight_here(slot)
        if above:
            weight(slot, 0, 96, down)
        else:
            weight(slot, 96, 32, up)

    def weight_pair(row):
        block = wb.at[pl.ds(4 * row, 4), :, half]
        remote(block, block, pair_send, pair_recv.at[row], other, sp).start()

    def grad_attn(row):
        arrived(wb.at[pl.ds(4 * row, 4), :, other_half], pair_recv.at[row])

        def one(i, _):
            i = 2 * row + i
            w = wb[pl.ds(2 * i, 2)].reshape(TOK, 3072)
            g = lax.dot_general(w, ds[...], NT, preferred_element_type=F32)
            gt[pl.ds(pl.multiple_of(i * TOK, TOK), TOK), :] = g.astype(BF)
            return 0

        lax.fori_loop(0, 2, one, 0)

    def spread(slot, j, first, rows, send, to):
        block = aa.at[slot, pl.ds(j * 512 + first, rows)]
        remote(block, block, send, a_recv.at[slot, j], to, sp).start()

    def spread_here(slot, j):
        arrived(aa.at[slot, pl.ds(j * 512, 512)], a_recv.at[slot, j])

    def spread_own(j):
        for i, to in enumerate((y_up, y_down, other)):
            spread(dp, j, 0, 512, a_send.at[i], to)

    def spread_on(j):
        spread_here(y_down, j)
        spread(y_down, j, 0, 256, a_send.at[3], y_up)
        spread(y_down, j, 0, 512, a_send.at[4], other)
        spread_here(y_up, j)
        spread(y_up, j, 256, 256, a_send.at[5], y_down)
        spread(y_up, j, 0, 512, a_send.at[6], other)

    def spread_far(j):
        spread_here(y_far, j)
        spread(y_far, j, 0, 512, a_send.at[7], other)

    diagonal = lax.broadcasted_iota(jnp.int32, (32, 32), 0) == lax.broadcasted_iota(jnp.int32, (32, 32), 1)
    slot_of = lax.broadcasted_iota(jnp.int32, (32, 128), 1)
    listed = jnp.full((32, 128), -100, jnp.int32)
    for i in range(8):
        row = jnp.where(cnt_ref[...] > i, list_ref[i : i + 1, :], -100)
        listed = jnp.where(slot_of == i, jnp.max(jnp.where(diagonal, row, -100), axis=1, keepdims=True), listed)
    raw[sp] = listed

    for copy in loads[:3]:
        copy.wait()
    for dx in (1, 3, 2):
        weight_quarter(sp, q_recv.at[sp], dp, sp_at(z, x + dx))
    first, *others = chunks(z + 1)
    kv_up(first).start()
    kv_rows(order[0], True)
    weight_z(sp)
    for j in others:
        kv_up(j).start()
    for r in range(1, 16):
        first_out.go(raw.at[sp], raw.at[sp], l_recv, dp, (sp + r) % 16)

    q_pos = sp * TOK + lax.broadcasted_iota(jnp.int32, (1, TOK), 1)
    begin = jnp.zeros((1, TOK), jnp.int32)
    start = jnp.int32(0)
    for i in range(16):
        begin = jnp.where(q_pos >= start, start, begin)
        start = start + len_ref[0, i]

    def mask(b, _):
        rows = pl.ds(pl.multiple_of(b * SIZE, SIZE), SIZE)
        k_pos = (sp - HALO) * TOK + b * SIZE + lax.broadcasted_iota(jnp.int32, (SIZE, TOK), 0)
        bias[rows, :] = jnp.where((k_pos <= q_pos) & (k_pos >= begin), 0.0, NEG)
        return 0

    lax.fori_loop(0, KB, mask, 0)

    for dx in (1, 3, 2):
        weight_quarter_here(sp_at(z, x + dx))
    kv_rows(order[1], True)
    kv_here(0, order[0])
    kv_rows(order[0], False)
    for dx in (1, 3, 2):
        weight_rest_here(sp_at(z, x + dx))
        weight_z(sp_at(z, x + dx))
    weight_pair(z)
    for r in (2, 6, 4, 1, 3, 5, 7):
        to = (dp + r) % 8
        first_out.go(d_ref.at[:, lanes_of(to, PART)], db.at[dp], d_recv, to, sp)
    kv_here(0, order[1])
    kv_rows(order[1], False)
    kv_rows(order[2], True)
    arrived(raw.at[pl.ds(0, 15)], l_recv)

    def list_terms(h, _):
        ids = 2 * sp - 2 * HALO + lax.broadcasted_iota(jnp.int32, (16, 128), 0)
        for i in range(2):
            found = jnp.where(raw[h, pl.ds(2 * sp + i, 1), :] == ids, 0.0, NEG)
            found = jnp.max(found, axis=1, keepdims=True)
            lb[h, :, i * SIZE : (i + 1) * SIZE] = jnp.broadcast_to(found, (16, SIZE))
        return 0

    lax.fori_loop(0, 16, list_terms, 0)
    for copy in loads[3:]:
        copy.wait()
    kv_here(0, order[2])
    kv_rows(order[2], False)
    kv_rows(order[3], True)
    grad_attn(z)

    def forward(c, _):
        forward_heads(c, qs, band, lb, bias, pb, rb, aa, an, dp)
        return 0

    def backward(c, _):
        backward_heads(c, qs, band, pb, rb, aa, gt, dp)
        cols = lanes_of(c, SIZE)
        for k in (2, 1, 3):
            remote(
                band.at[:, 4 - k, :, cols], back.at[k - 1, :, :, cols], row_send.at[k - 1], row_recv.at[k - 1, c], dp, sp_at(z, x - k)
            ).start()
        return 0

    def backward_chunk(j, between=None):
        cols = lanes_of(j, 256)
        for k in range(4):
            remote(band.at[:, 0, :, cols], band.at[:, 0, :, cols], kv_send.at[k, j], kv_send.at[k, j], dp, up).wait_send()
        if between is None:
            lax.fori_loop(2 * j, 2 * j + 2, backward, 0)
        else:
            lax.fori_loop(2 * j, 2 * j + 1, backward, 0)
            between()
            lax.fori_loop(2 * j + 1, 2 * j + 2, backward, 0)

    def spread_in(j):
        for r in range(4):
            spread_here(dp_at(y + r, 1 - core), j)

    def weight_grad(j):
        rows = pl.ds(pl.multiple_of(j * 512, 512), 512)
        total = jnp.zeros((512, PART), F32)
        for e in range(8):
            total = total + jnp.dot(aa[e, rows, :], db[e], preferred_element_type=F32)
        gw[pl.ds(4 * j, 4)] = total.astype(BF).reshape(4, 128, PART)

    def scatter_z(j):
        k = (z - j + 4) % 4 - 1
        remote(gw.at[pl.ds(4 * j, 4)], rs.at[pl.ds(4 * k, 4)], rs_send.at[0], rs_recv.at[0], dp, sp_at(j, x)).start()

    def kv_chunk(j):
        for slot in (3, 1, 2):
            kv_here(slot, j)

    def forward_chunk(j):
        lax.fori_loop(2 * j, 2 * j + 2, forward, 0)
        spread_own(j)

    own_row, row_above, row_below, row_far = order

    def scatter(j):
        spread_in(j)
        weight_grad(j)
        if j is not own_row:
            scatter_z(j)

    kv_chunk(own_row)
    forward_chunk(own_row)
    kv_here(0, row_far)
    kv_rows(row_far, False)
    backward_chunk(own_row)
    weight_relay(0, True)
    weight_relay(0, False)

    kv_chunk(row_above)
    forward_chunk(row_above)
    for dx in (1, 3):
        weight_relay(dx, True)
        weight_relay(dx, False)
    spread_on(own_row)

    kv_chunk(row_below)
    forward_chunk(row_below)
    weight_relay(2, True)
    weight_pair(row_above)
    weight_relay(2, False)
    weight_pair(row_below)
    grad_attn(row_above)
    backward_chunk(row_above)
    spread_on(row_above)
    spread_far(own_row)
    grad_attn(row_below)
    backward_chunk(row_below)
    spread_on(row_below)
    spread_far(row_above)
    arrived(db.at[pl.ds(0, 7)], d_recv)
    scatter(own_row)
    scatter(row_above)
    for i in range(4):
        weight_here(4 * row_far + i)
    weight_pair(row_far)

    kv_chunk(row_far)
    forward_chunk(row_far)
    spread_far(row_below)
    grad_attn(row_far)
    scatter(row_below)
    backward_chunk(row_far, lambda: spread_on(row_far))
    dq_out = pltpu.make_async_copy(qs, dq_ref, local.at[7])
    dq_out.start()
    spread_far(row_far)
    scatter(row_far)

    keep = [jnp.where(x + k < 4, 1.0, 0.0).astype(F32) for k in (1, 2, 3)]

    def row_sums(j):
        def one(c, _):
            cols = lanes_of(c, SIZE)
            for k in range(3):
                arrived(back.at[k, :, :, cols], row_recv.at[k, c])
            below = band[:, 0, :, cols].astype(F32)
            here = band[:, 4, :, cols].astype(F32)
            for k in range(3):
                got = back[k, :, :, cols].astype(F32)
                here = here + got * keep[k]
                below = below + got * (1.0 - keep[k])
            band[:, 0, :, cols] = below.astype(BF)
            band[:, 4, :, cols] = here.astype(BF)
            for i in range(2):
                remote(band.at[i, 0, :, cols], (gk_z_ref, gv_z_ref)[i].at[:, cols], z_send, z_recv, dp, down).start()
            return 0

        lax.fori_loop(2 * j, 2 * j + 2, one, 0)

    def project(i, _):
        cols = lanes_of(i, 512)
        w = wb[:, :, cols].reshape(2048, 512)
        ds[:, cols] = jnp.dot(an[...], w, preferred_element_type=F32).astype(BF)
        return 0

    lax.fori_loop(0, 6, project, 0)
    lo_out = pltpu.make_async_copy(ds, lo_ref, local.at[8])
    lo_out.start()

    row_sums(own_row)
    arrived(rs.at[pl.ds(0, 12)], rs_recv.at[0])

    def z_sums(i, _):
        total = gw[4 * z + i].astype(F32)
        for t in range(3):
            total = total + rs[4 * t + i].astype(F32)
        rs[12 + i] = total.astype(BF)

        @pl.when(i != x)
        def _():
            k = (x - i + 4) % 4 - 1
            remote(rs.at[12 + i], rx.at[k], rs_send.at[1], rs_recv.at[1], dp, sp_at(z, i)).start()

        return 0

    lax.fori_loop(0, 4, z_sums, 0)
    row_sums(row_above)
    row_sums(row_below)
    arrived(rx, rs_recv.at[1])
    total = rs[12 + x].astype(F32)
    for r in range(3):
        total = total + rx[r].astype(F32)
    gsum[...] = total.astype(BF)
    g_out = Sends(g_send)

    def g_block(e):
        return gb_ref.at[:, lanes_of(e, PART)]

    for to in (y_far, y_up, y_down, other):
        g_out.go(gsum, g_block(dp), g_recv.at[dp], to, sp)
    own_sum = pltpu.make_async_copy(gsum, gb_ref.at[:, lanes_of(dp, PART)], local.at[9])
    own_sum.start()

    row_sums(row_far)
    kv_outs = [
        pltpu.make_async_copy(band.at[0, 4], gk_ref, local.at[10]),
        pltpu.make_async_copy(band.at[1, 4], gv_ref, local.at[2]),
    ]
    for copy in kv_outs:
        copy.start()
    for slot in (y_up, y_down, y_far):
        arrived(g_block(slot), g_recv.at[slot])
        g_out.go(g_block(slot), g_block(slot), g_recv.at[slot], other, sp)
    for r in range(4):
        slot = dp_at(y + r, 1 - core)
        arrived(g_block(slot), g_recv.at[slot])
    arrived(band.at[:, 0], z_recv)
    first_out.finish()
    w_out.finish()
    some = wb.at[:, :, half]
    remote(some, some, pair_send, pair_send, other, sp).wait_send()
    for i in range(8):
        some = aa.at[dp, pl.ds(0, 1024 if i in (3, 5) else 2048)]
        remote(some, some, a_send.at[i], a_send.at[i], other, sp).wait_send()
    for k in range(3):
        remote(back.at[k], back.at[k], row_send.at[k], row_send.at[k], dp, up).wait_send()
    remote(band.at[:, 0], band.at[:, 0], z_send, z_send, dp, down).wait_send()
    remote(rs.at[pl.ds(0, 12)], rs.at[pl.ds(0, 12)], rs_send.at[0], rs_send.at[0], dp, up).wait_send()
    remote(rx, rx, rs_send.at[1], rs_send.at[1], dp, up).wait_send()
    g_out.finish()
    for copy in (dq_out, lo_out, own_sum, *kv_outs):
        copy.wait()


def call_layer(q, k, v, lists, counts, lengths, w, d):
    vmem = pltpu.VMEM
    return pl.pallas_call(
        layer_kernel,
        in_specs=[ANY] * 3
        + [pl.BlockSpec(memory_space=vmem)] * 2
        + [pl.BlockSpec(memory_space=pltpu.SMEM)]
        + [ANY] * 2,
        out_specs=[ANY] * 7,
        out_shape=[
            jax.ShapeDtypeStruct((TOK, 3072), BF),
            jax.ShapeDtypeStruct((TOK, 2048), BF),
            jax.ShapeDtypeStruct((TOK, 1024), BF),
            jax.ShapeDtypeStruct((TOK, 1024), BF),
            jax.ShapeDtypeStruct((TOK, 1024), BF),
            jax.ShapeDtypeStruct((TOK, 1024), BF),
            jax.ShapeDtypeStruct((128, 3072), BF),
        ],
        scratch_shapes=[
            vmem((2, 5, TOK, 1024), BF),
            vmem((16, 32, 128), jnp.int32),
            vmem((16, 16, TOK), F32),
            vmem((16, 128, 3072), BF),
            vmem((8, TOK, PART), BF),
            vmem((TOK, 2048), BF),
            vmem((TOK, 3072), BF),
            vmem((BAND, TOK), F32),
            vmem((16, BAND, TOK), BF),
            vmem((16, 8, TOK), F32),
            vmem((8, 2048, TOK), BF),
            vmem((TOK, 2048), BF),
            vmem((2048, TOK), BF),
            vmem((3, 2, TOK, 1024), BF),
            vmem((16, 128, PART), BF),
            vmem((16, 128, PART), BF),
            vmem((3, 128, PART), BF),
            vmem((128, PART), BF),
            DMA((11,)),
            DMA((4, 4)),
            DMA((4, 4)),
            DMA((28,)),
            DMA((16,)),
            DMA((16,)),
            DMA,
            DMA((4,)),
            DMA((22,)),
            DMA,
            DMA,
            DMA((8,)),
            DMA((8, 4)),
            DMA((3,)),
            DMA((3, 8)),
            DMA,
            DMA,
            DMA((2,)),
            DMA((2,)),
            DMA((7,)),
            DMA((8,)),
        ],
        compiler_params=pltpu.CompilerParams(collective_id=0, has_side_effects=True, vmem_limit_bytes=60 * 2**20),
        cost_estimate=pl.CostEstimate(flops=27 * 10**9, bytes_accessed=20 * 10**6, transcendentals=6 * 10**6),
    )(q, k, v, lists, counts, lengths, w, d)


def per_device(queries, keys, values, key_blocks, block_counts, doc_lengths, out_weight, d_out):
    layer_out, grad_q, grad_k, grad_v, more_k, more_v, grad_all = call_layer(
        queries[0], keys[0], values[0], key_blocks[0, 0].T, block_counts[0], doc_lengths, out_weight, d_out[0]
    )
    grad_k = (grad_k.astype(F32) + more_k.astype(F32)).astype(BF)
    grad_v = (grad_v.astype(F32) + more_v.astype(F32)).astype(BF)
    grad_weight = grad_all.astype(F32)
    tokens = lax.axis_size("dp") * lax.axis_size("sp") * TOK
    grad_weight = grad_weight * (1.0 / math.sqrt(tokens))
    return (layer_out[None], grad_q[None], grad_k[None], grad_v[None], grad_weight)


def solution(mesh):
    in_specs = (
        P("dp", "sp", None),
        P("dp", "sp", None),
        P("dp", "sp", None),
        P("dp", "sp", None, None),
        P("dp", "sp", None),
        P("dp", None),
        P("sp", None),
        P("dp", "sp", None),
    )
    out_specs = (
        P("dp", "sp", None),
        P("dp", "sp", None),
        P("dp", "sp", None),
        P("dp", "sp", None),
        P("sp", None),
    )
    return jax.shard_map(per_device, mesh=mesh, in_specs=in_specs, out_specs=out_specs, check_vma=False)
```

```python
import math

import jax
import jax.numpy as jnp
from jax import lax
from jax.experimental import pallas as pl
from jax.experimental.pallas import tpu as pltpu
from jax.sharding import PartitionSpec as P

SIZE = 128
TOK = 256
HALO = 4
BAND = (HALO + 1) * TOK
KB = BAND // SIZE
NEG = -1e30
BF = jnp.bfloat16
F32 = jnp.float32
NT = (((1,), (1,)), ((), ()))
TN = (((0,), (0,)), ((), ()))


MESH = pl.DeviceIdType.MESH
PART = 384
HALF = 1536


def place():
    dp = lax.axis_index("dp")
    sp = lax.axis_index("sp")
    return dp, sp, sp // 4, sp % 4


def sp_at(z, x):
    return (z + 4) % 4 * 4 + (x + 4) % 4


def dp_at(y, core):
    return (y + 4) % 4 * 2 + core


def greet():
    dp, sp, _, _ = place()
    barrier = pltpu.get_barrier_semaphore()
    for r in range(1, 16):
        pl.semaphore_signal(barrier, inc=1, device_id=(dp, (sp + r) % 16), device_id_type=MESH)
    for r in range(1, 8):
        pl.semaphore_signal(barrier, inc=1, device_id=((dp + r) % 8, sp), device_id_type=MESH)
    pl.semaphore_wait(barrier, 22)


def remote(src, dst, send, recv, dp, sp):
    return pltpu.make_async_remote_copy(
        src_ref=src, dst_ref=dst, send_sem=send, recv_sem=recv, device_id=(dp, sp), device_id_type=MESH
    )


class Sends:
    def __init__(self, sems):
        self.sems = sems
        self.started = []

    def go(self, src, dst, recv, dp, sp, when=None):
        copy = remote(src, dst, self.sems.at[len(self.started)], recv, dp, sp)
        self.started.append((copy, when))
        if when is None:
            copy.start()
        else:
            pl.when(when)(copy.start)

    def finish(self):
        for copy, when in self.started:
            if when is None:
                copy.wait_send()
            else:
                pl.when(when)(copy.wait_send)


def arrived(dst, recv):
    dp, sp, _, _ = place()
    remote(dst, dst, recv, recv, dp, sp).wait_recv()


SCALE = 1.0 / math.sqrt(SIZE)
FACTOR = SCALE * math.log2(math.e)
ANY = pl.BlockSpec(memory_space=pl.ANY)
DMA = pltpu.SemaphoreType.DMA


def lanes_of(i, width):
    return pl.ds(pl.multiple_of(i * width, width), width)


def forward_heads(c, qs, band, lb, bias, pb, rb, aa, an, dp):
    cols = lanes_of(c, SIZE)
    for h in range(2):
        head = 2 * c + h
        lanes = lanes_of(head, SIZE)
        q = qs[:, lanes]
        scores = []
        top = None
        for b in range(KB):
            k = band[0, b // 2, pl.ds(b % 2 * SIZE, SIZE), cols]
            s = lax.dot_general(k, q, NT, preferred_element_type=F32)
            s = s + bias[b * SIZE : (b + 1) * SIZE, :] + lb[head, b : b + 1, :]
            scores.append(s)
            t = jnp.max(s, axis=0, keepdims=True)
            top = t if top is None else jnp.maximum(top, t)
        total = jnp.zeros((1, TOK), F32)
        for b in range(KB):
            p = jnp.exp2((scores[b] - top) * FACTOR)
            total = total + jnp.sum(p, axis=0, keepdims=True)
            pb[head, b * SIZE : (b + 1) * SIZE, :] = p.astype(BF)
        v = band[1, :, :, cols].reshape(BAND, SIZE)
        out = lax.dot_general(v, pb[head], TN, preferred_element_type=F32)
        inverse = 1.0 / total
        rb[head] = jnp.broadcast_to(inverse, (8, TOK))
        out = out * inverse
        aa[dp, lanes, :] = out.astype(BF)
        an[:, lanes] = out.T.astype(BF)


def backward_heads(c, qs, band, pb, rb, aa, gt, dp):
    cols = lanes_of(c, SIZE)
    k = band[0, :, :, cols].reshape(BAND, SIZE)
    v = band[1, :, :, cols].reshape(BAND, SIZE)
    dk = jnp.zeros((BAND, SIZE), F32)
    dv = jnp.zeros((BAND, SIZE), F32)
    for h in range(2):
        head = 2 * c + h
        lanes = lanes_of(head, SIZE)
        inverse = rb[head, 0:1, :]
        g_t = gt[lanes, :].astype(F32)
        delta = jnp.sum(g_t * aa[dp, lanes, :].astype(F32), axis=0, keepdims=True) * inverse
        g_t = g_t * inverse
        g = g_t.T.astype(BF)
        grad_p = jnp.dot(v, g_t.astype(BF), preferred_element_type=F32)
        p = pb[head]
        grad_s = (p.astype(F32) * (grad_p - delta)).astype(BF)
        dq_t = lax.dot_general(k, grad_s, TN, preferred_element_type=F32)
        dk = dk + jnp.dot(grad_s, qs[:, lanes], preferred_element_type=F32)
        dv = dv + jnp.dot(p, g, preferred_element_type=F32)
        qs[:, lanes] = (dq_t * SCALE).T.astype(BF)
    band[0, :, :, cols] = (dk * SCALE).astype(BF).reshape(5, TOK, SIZE)
    band[1, :, :, cols] = dv.astype(BF).reshape(5, TOK, SIZE)


def layer_kernel(
    q_ref, k_ref, v_ref, list_ref, cnt_ref, len_ref, w_ref, d_ref,
    lo_ref, dq_ref, gk_ref, gv_ref, gk_z_ref, gv_z_ref, gb_ref,
    band, raw, lb, wb, db, qs, ds, bias, pb, rb, aa, an, gt, back, gw, rs, rx, gsum,
    local, kv_send, kv_recv, w_send, w_recv, q_recv, pair_send, pair_recv, first_send, l_recv, d_recv,
    a_send, a_recv, row_send, row_recv, z_send, z_recv, rs_send, rs_recv, g_send, g_recv,
):
    dp, sp, z, x = place()
    y, core = dp // 2, dp % 2
    other = dp_at(y, 1 - core)
    loads = [
        pltpu.make_async_copy(k_ref, band.at[0, 4], local.at[0]),
        pltpu.make_async_copy(v_ref, band.at[1, 4], local.at[1]),
        pltpu.make_async_copy(w_ref.at[:, lanes_of(core, HALF)], wb.at[sp, :, lanes_of(core, HALF)], local.at[3]),
        pltpu.make_async_copy(d_ref.at[:, lanes_of(dp, PART)], db.at[dp], local.at[4]),
        pltpu.make_async_copy(q_ref, qs, local.at[5]),
        pltpu.make_async_copy(d_ref, ds, local.at[6]),
    ]
    for copy in loads:
        copy.start()
    greet()
    def chunks(row):
        return [(row + i) % 4 for i in (0, 1, 3, 2)]

    order = chunks(z)
    first_out = Sends(first_send)
    up, down = sp_at(z + 1, x), sp_at(z - 1, x)
    y_up, y_down, y_far = dp_at(y + 1, core), dp_at(y - 1, core), dp_at(y + 2, core)

    def kv_up(j):
        cols = lanes_of(j, 256)
        return remote(band.at[:, 4, :, cols], band.at[:, 0, :, cols], kv_send.at[0, j], kv_recv.at[0, j], dp, up)

    def kv_row(k, j):
        cols = lanes_of(j, 256)
        src = band.at[:, jnp.where(x + k < 4, 4, 0), :, cols]
        return remote(src, band.at[:, 4 - k, :, cols], kv_send.at[k, j], kv_recv.at[4 - k, j], dp, sp_at(z, x + k))

    def kv_rows(j, mine):
        for k in (2, 1, 3):
            pl.when((x + k < 4) if mine else (x + k >= 4))(kv_row(k, j).start)

    def kv_here(slot, j):
        arrived(band.at[:, slot, :, lanes_of(j, 256)], kv_recv.at[slot, j])

    half, other_half = lanes_of(core, HALF), lanes_of(1 - core, HALF)
    w_out = Sends(w_send)

    def weight(slot, first, rows, to):
        block = wb.at[slot, pl.ds(first, rows), half]
        w_out.go(block, block, w_recv.at[slot], dp, to)

    def weight_here(slot):
        arrived(wb.at[slot, :, half], w_recv.at[slot])

    def weight_quarter(slot, recv, to_dp, to_sp):
        block = wb.at[slot, pl.ds(pl.multiple_of(32 * y, 32), 32), half]
        w_out.go(block, block, recv, to_dp, to_sp)

    def weight_quarter_here(slot):
        arrived(wb.at[slot, pl.ds(0, 32), half], q_recv.at[slot])
        for dy in (1, 3, 2):
            weight_quarter(slot, w_recv.at[slot], dp_at(y + dy, core), sp)

    def weight_rest_here(slot):
        arrived(wb.at[slot, pl.ds(0, 96), half], w_recv.at[slot])

    def weight_z(slot):
        weight(slot, 0, 128, up)
        weight(slot, 0, 128, down)

    def weight_relay(dx, above):
        slot = sp_at(z + 1 if above else z - 1, x + dx)
        weight_here(slot)
        if above:
            weight(slot, 0, 96, down)
        else:
            weight(slot, 96, 32, up)

    def weight_pair(row):
        block = wb.at[pl.ds(4 * row, 4), :, half]
        remote(block, block, pair_send, pair_recv.at[row], other, sp).start()

    def grad_attn(row):
        arrived(wb.at[pl.ds(4 * row, 4), :, other_half], pair_recv.at[row])

        def one(i, _):
            i = 2 * row + i
            w = wb[pl.ds(2 * i, 2)].reshape(TOK, 3072)
            g = lax.dot_general(w, ds[...], NT, preferred_element_type=F32)
            gt[pl.ds(pl.multiple_of(i * TOK, TOK), TOK), :] = g.astype(BF)
            return 0

        lax.fori_loop(0, 2, one, 0)

    def spread(slot, j, first, rows, send, to):
        block = aa.at[slot, pl.ds(j * 512 + first, rows)]
        remote(block, block, send, a_recv.at[slot, j], to, sp).start()

    def spread_here(slot, j):
        arrived(aa.at[slot, pl.ds(j * 512, 512)], a_recv.at[slot, j])

    def spread_own(c):
        for i, to in enumerate((y_up, y_down, other)):
            spread(dp, c // 2, c % 2 * 256, 256, a_send.at[i], to)

    def spread_on(j):
        spread_here(y_down, j)
        spread(y_down, j, 0, 256, a_send.at[3], y_up)
        spread(y_down, j, 0, 512, a_send.at[4], other)
        spread_here(y_up, j)
        spread(y_up, j, 256, 256, a_send.at[5], y_down)
        spread(y_up, j, 0, 512, a_send.at[6], other)

    def spread_far(j):
        spread_here(y_far, j)
        spread(y_far, j, 0, 512, a_send.at[7], other)

    diagonal = lax.broadcasted_iota(jnp.int32, (32, 32), 0) == lax.broadcasted_iota(jnp.int32, (32, 32), 1)
    slot_of = lax.broadcasted_iota(jnp.int32, (32, 128), 1)
    listed = jnp.full((32, 128), -100, jnp.int32)
    for i in range(8):
        row = jnp.where(cnt_ref[...] > i, list_ref[i : i + 1, :], -100)
        listed = jnp.where(slot_of == i, jnp.max(jnp.where(diagonal, row, -100), axis=1, keepdims=True), listed)
    raw[sp] = listed

    for copy in loads[:3]:
        copy.wait()
    for dx in (1, 3, 2):
        weight_quarter(sp, q_recv.at[sp], dp, sp_at(z, x + dx))
    first, *others = chunks(z + 1)
    kv_up(first).start()
    kv_rows(order[0], True)
    weight_z(sp)
    for j in others:
        kv_up(j).start()
    for r in range(1, 16):
        first_out.go(raw.at[sp], raw.at[sp], l_recv, dp, (sp + r) % 16)

    q_pos = sp * TOK + lax.broadcasted_iota(jnp.int32, (1, TOK), 1)
    begin = jnp.zeros((1, TOK), jnp.int32)
    start = jnp.int32(0)
    for i in range(16):
        begin = jnp.where(q_pos >= start, start, begin)
        start = start + len_ref[0, i]

    def mask(b, _):
        rows = pl.ds(pl.multiple_of(b * SIZE, SIZE), SIZE)
        k_pos = (sp - HALO) * TOK + b * SIZE + lax.broadcasted_iota(jnp.int32, (SIZE, TOK), 0)
        bias[rows, :] = jnp.where((k_pos <= q_pos) & (k_pos >= begin), 0.0, NEG)
        return 0

    lax.fori_loop(0, KB, mask, 0)

    for dx in (1, 3, 2):
        weight_quarter_here(sp_at(z, x + dx))
    kv_rows(order[1], True)
    kv_here(0, order[0])
    kv_rows(order[0], False)
    for dx in (1, 3, 2):
        weight_rest_here(sp_at(z, x + dx))
        weight_z(sp_at(z, x + dx))
    weight_pair(z)
    for r in (2, 6, 4, 1, 3, 5, 7):
        to = (dp + r) % 8
        first_out.go(d_ref.at[:, lanes_of(to, PART)], db.at[dp], d_recv, to, sp)
    kv_here(0, order[1])
    kv_rows(order[1], False)
    kv_rows(order[2], True)
    arrived(raw.at[pl.ds(0, 15)], l_recv)

    def list_terms(h, _):
        ids = 2 * sp - 2 * HALO + lax.broadcasted_iota(jnp.int32, (16, 128), 0)
        for i in range(2):
            found = jnp.where(raw[h, pl.ds(2 * sp + i, 1), :] == ids, 0.0, NEG)
            found = jnp.max(found, axis=1, keepdims=True)
            lb[h, :, i * SIZE : (i + 1) * SIZE] = jnp.broadcast_to(found, (16, SIZE))
        return 0

    lax.fori_loop(0, 16, list_terms, 0)
    for copy in loads[3:]:
        copy.wait()
    kv_here(0, order[2])
    kv_rows(order[2], False)
    kv_rows(order[3], True)
    grad_attn(z)

    def forward(c, _):
        forward_heads(c, qs, band, lb, bias, pb, rb, aa, an, dp)
        spread_own(c)
        return 0

    def backward(c, _):
        backward_heads(c, qs, band, pb, rb, aa, gt, dp)
        cols = lanes_of(c, SIZE)
        for k in (2, 1, 3):
            remote(
                band.at[:, 4 - k, :, cols], back.at[k - 1, :, :, cols], row_send.at[k - 1], row_recv.at[k - 1, c], dp, sp_at(z, x - k)
            ).start()
        return 0

    def backward_chunk(j, between=None):
        cols = lanes_of(j, 256)
        for k in range(4):
            remote(band.at[:, 0, :, cols], band.at[:, 0, :, cols], kv_send.at[k, j], kv_send.at[k, j], dp, up).wait_send()
        if between is None:
            lax.fori_loop(2 * j, 2 * j + 2, backward, 0)
        else:
            lax.fori_loop(2 * j, 2 * j + 1, backward, 0)
            between()
            lax.fori_loop(2 * j + 1, 2 * j + 2, backward, 0)

    def spread_in(j):
        for r in range(4):
            spread_here(dp_at(y + r, 1 - core), j)

    def weight_grad(j):
        rows = pl.ds(pl.multiple_of(j * 512, 512), 512)
        total = jnp.zeros((512, PART), F32)
        for e in range(8):
            total = total + jnp.dot(aa[e, rows, :], db[e], preferred_element_type=F32)
        gw[pl.ds(4 * j, 4)] = total.astype(BF).reshape(4, 128, PART)

    def scatter_z(j):
        k = (z - j + 4) % 4 - 1
        remote(gw.at[pl.ds(4 * j, 4)], rs.at[pl.ds(4 * k, 4)], rs_send.at[0], rs_recv.at[0], dp, sp_at(j, x)).start()

    def kv_chunk(j):
        for slot in (3, 1, 2):
            kv_here(slot, j)

    def forward_chunk(j):
        lax.fori_loop(2 * j, 2 * j + 2, forward, 0)

    own_row, row_above, row_below, row_far = order

    def scatter(j):
        spread_in(j)
        weight_grad(j)
        if j is not own_row:
            scatter_z(j)

    kv_chunk(own_row)
    forward_chunk(own_row)
    kv_here(0, row_far)
    kv_rows(row_far, False)
    backward_chunk(own_row)
    weight_relay(0, True)
    weight_relay(0, False)

    kv_chunk(row_above)
    forward_chunk(row_above)
    for dx in (1, 3):
        weight_relay(dx, True)
        weight_relay(dx, False)
    spread_on(own_row)

    kv_chunk(row_below)
    forward_chunk(row_below)
    weight_relay(2, True)
    weight_pair(row_above)
    weight_relay(2, False)
    weight_pair(row_below)
    grad_attn(row_above)
    backward_chunk(row_above)
    spread_on(row_above)
    spread_far(own_row)
    grad_attn(row_below)
    backward_chunk(row_below)
    spread_on(row_below)
    spread_far(row_above)
    for i in range(4):
        weight_here(4 * row_far + i)
    weight_pair(row_far)

    kv_chunk(row_far)
    forward_chunk(row_far)
    arrived(db.at[pl.ds(0, 7)], d_recv)
    scatter(own_row)
    scatter(row_above)
    spread_far(row_below)
    grad_attn(row_far)
    scatter(row_below)
    backward_chunk(row_far, lambda: spread_on(row_far))
    dq_out = pltpu.make_async_copy(qs, dq_ref, local.at[7])
    dq_out.start()
    spread_far(row_far)
    scatter(row_far)

    keep = [jnp.where(x + k < 4, 1.0, 0.0).astype(F32) for k in (1, 2, 3)]

    def row_sums(j):
        def one(c, _):
            cols = lanes_of(c, SIZE)
            for k in range(3):
                arrived(back.at[k, :, :, cols], row_recv.at[k, c])
            below = band[:, 0, :, cols].astype(F32)
            here = band[:, 4, :, cols].astype(F32)
            for k in range(3):
                got = back[k, :, :, cols].astype(F32)
                here = here + got * keep[k]
                below = below + got * (1.0 - keep[k])
            band[:, 0, :, cols] = below.astype(BF)
            band[:, 4, :, cols] = here.astype(BF)
            for i in range(2):
                remote(band.at[i, 0, :, cols], (gk_z_ref, gv_z_ref)[i].at[:, cols], z_send, z_recv, dp, down).start()
            return 0

        lax.fori_loop(2 * j, 2 * j + 2, one, 0)

    def project(i, _):
        cols = lanes_of(i, 512)
        w = wb[:, :, cols].reshape(2048, 512)
        ds[:, cols] = jnp.dot(an[...], w, preferred_element_type=F32).astype(BF)
        return 0

    lax.fori_loop(0, 6, project, 0)
    lo_out = pltpu.make_async_copy(ds, lo_ref, local.at[8])
    lo_out.start()

    row_sums(own_row)
    arrived(rs.at[pl.ds(0, 12)], rs_recv.at[0])

    def z_sums(i, _):
        total = gw[4 * z + i].astype(F32)
        for t in range(3):
            total = total + rs[4 * t + i].astype(F32)
        rs[12 + i] = total.astype(BF)

        @pl.when(i != x)
        def _():
            k = (x - i + 4) % 4 - 1
            remote(rs.at[12 + i], rx.at[k], rs_send.at[1], rs_recv.at[1], dp, sp_at(z, i)).start()

        return 0

    lax.fori_loop(0, 4, z_sums, 0)
    row_sums(row_above)
    row_sums(row_below)
    arrived(rx, rs_recv.at[1])
    total = rs[12 + x].astype(F32)
    for r in range(3):
        total = total + rx[r].astype(F32)
    gsum[...] = total.astype(BF)
    g_out = Sends(g_send)

    def g_block(e):
        return gb_ref.at[:, lanes_of(e, PART)]

    for to in (y_far, y_up, y_down, other):
        g_out.go(gsum, g_block(dp), g_recv.at[dp], to, sp)
    own_sum = pltpu.make_async_copy(gsum, gb_ref.at[:, lanes_of(dp, PART)], local.at[9])
    own_sum.start()

    row_sums(row_far)
    kv_outs = [
        pltpu.make_async_copy(band.at[0, 4], gk_ref, local.at[10]),
        pltpu.make_async_copy(band.at[1, 4], gv_ref, local.at[2]),
    ]
    for copy in kv_outs:
        copy.start()
    for slot in (y_up, y_down, y_far):
        arrived(g_block(slot), g_recv.at[slot])
        g_out.go(g_block(slot), g_block(slot), g_recv.at[slot], other, sp)
    for r in range(4):
        slot = dp_at(y + r, 1 - core)
        arrived(g_block(slot), g_recv.at[slot])
    arrived(band.at[:, 0], z_recv)
    first_out.finish()
    w_out.finish()
    some = wb.at[:, :, half]
    remote(some, some, pair_send, pair_send, other, sp).wait_send()
    for i in range(8):
        some = aa.at[dp, pl.ds(0, 1024 if i in (3, 5) else 2048)]
        remote(some, some, a_send.at[i], a_send.at[i], other, sp).wait_send()
    for k in range(3):
        remote(back.at[k], back.at[k], row_send.at[k], row_send.at[k], dp, up).wait_send()
    remote(band.at[:, 0], band.at[:, 0], z_send, z_send, dp, down).wait_send()
    remote(rs.at[pl.ds(0, 12)], rs.at[pl.ds(0, 12)], rs_send.at[0], rs_send.at[0], dp, up).wait_send()
    remote(rx, rx, rs_send.at[1], rs_send.at[1], dp, up).wait_send()
    g_out.finish()
    for copy in (dq_out, lo_out, own_sum, *kv_outs):
        copy.wait()


def call_layer(q, k, v, lists, counts, lengths, w, d):
    vmem = pltpu.VMEM
    return pl.pallas_call(
        layer_kernel,
        in_specs=[ANY] * 3
        + [pl.BlockSpec(memory_space=vmem)] * 2
        + [pl.BlockSpec(memory_space=pltpu.SMEM)]
        + [ANY] * 2,
        out_specs=[ANY] * 7,
        out_shape=[
            jax.ShapeDtypeStruct((TOK, 3072), BF),
            jax.ShapeDtypeStruct((TOK, 2048), BF),
            jax.ShapeDtypeStruct((TOK, 1024), BF),
            jax.ShapeDtypeStruct((TOK, 1024), BF),
            jax.ShapeDtypeStruct((TOK, 1024), BF),
            jax.ShapeDtypeStruct((TOK, 1024), BF),
            jax.ShapeDtypeStruct((128, 3072), BF),
        ],
        scratch_shapes=[
            vmem((2, 5, TOK, 1024), BF),
            vmem((16, 32, 128), jnp.int32),
            vmem((16, 16, TOK), F32),
            vmem((16, 128, 3072), BF),
            vmem((8, TOK, PART), BF),
            vmem((TOK, 2048), BF),
            vmem((TOK, 3072), BF),
            vmem((BAND, TOK), F32),
            vmem((16, BAND, TOK), BF),
            vmem((16, 8, TOK), F32),
            vmem((8, 2048, TOK), BF),
            vmem((TOK, 2048), BF),
            vmem((2048, TOK), BF),
            vmem((3, 2, TOK, 1024), BF),
            vmem((16, 128, PART), BF),
            vmem((16, 128, PART), BF),
            vmem((3, 128, PART), BF),
            vmem((128, PART), BF),
            DMA((11,)),
            DMA((4, 4)),
            DMA((4, 4)),
            DMA((28,)),
            DMA((16,)),
            DMA((16,)),
            DMA,
            DMA((4,)),
            DMA((22,)),
            DMA,
            DMA,
            DMA((8,)),
            DMA((8, 4)),
            DMA((3,)),
            DMA((3, 8)),
            DMA,
            DMA,
            DMA((2,)),
            DMA((2,)),
            DMA((7,)),
            DMA((8,)),
        ],
        compiler_params=pltpu.CompilerParams(collective_id=0, has_side_effects=True, vmem_limit_bytes=60 * 2**20),
        cost_estimate=pl.CostEstimate(flops=27 * 10**9, bytes_accessed=20 * 10**6, transcendentals=6 * 10**6),
    )(q, k, v, lists, counts, lengths, w, d)


def per_device(queries, keys, values, key_blocks, block_counts, doc_lengths, out_weight, d_out):
    layer_out, grad_q, grad_k, grad_v, more_k, more_v, grad_all = call_layer(
        queries[0], keys[0], values[0], key_blocks[0, 0].T, block_counts[0], doc_lengths, out_weight, d_out[0]
    )
    grad_k = (grad_k.astype(F32) + more_k.astype(F32)).astype(BF)
    grad_v = (grad_v.astype(F32) + more_v.astype(F32)).astype(BF)
    grad_weight = grad_all.astype(F32)
    tokens = lax.axis_size("dp") * lax.axis_size("sp") * TOK
    grad_weight = grad_weight * (1.0 / math.sqrt(tokens))
    return (layer_out[None], grad_q[None], grad_k[None], grad_v[None], grad_weight)


def solution(mesh):
    in_specs = (
        P("dp", "sp", None),
        P("dp", "sp", None),
        P("dp", "sp", None),
        P("dp", "sp", None, None),
        P("dp", "sp", None),
        P("dp", None),
        P("sp", None),
        P("dp", "sp", None),
    )
    out_specs = (
        P("dp", "sp", None),
        P("dp", "sp", None),
        P("dp", "sp", None),
        P("dp", "sp", None),
        P("sp", None),
    )
    return jax.shard_map(per_device, mesh=mesh, in_specs=in_specs, out_specs=out_specs, check_vma=False)
```

```python
import math

import jax
import jax.numpy as jnp
from jax import lax
from jax.experimental import pallas as pl
from jax.experimental.pallas import tpu as pltpu
from jax.sharding import PartitionSpec as P

SIZE = 128
TOK = 256
HALO = 4
BAND = (HALO + 1) * TOK
KB = BAND // SIZE
NEG = -1e30
BF = jnp.bfloat16
F32 = jnp.float32
NT = (((1,), (1,)), ((), ()))
TN = (((0,), (0,)), ((), ()))


MESH = pl.DeviceIdType.MESH
PART = 384
HALF = 1536


def place():
    dp = lax.axis_index("dp")
    sp = lax.axis_index("sp")
    return dp, sp, sp // 4, sp % 4


def sp_at(z, x):
    return (z + 4) % 4 * 4 + (x + 4) % 4


def dp_at(y, core):
    return (y + 4) % 4 * 2 + core


def greet():
    dp, sp, _, _ = place()
    barrier = pltpu.get_barrier_semaphore()
    for r in range(1, 16):
        pl.semaphore_signal(barrier, inc=1, device_id=(dp, (sp + r) % 16), device_id_type=MESH)
    for r in range(1, 8):
        pl.semaphore_signal(barrier, inc=1, device_id=((dp + r) % 8, sp), device_id_type=MESH)
    pl.semaphore_wait(barrier, 22)


def remote(src, dst, send, recv, dp, sp):
    return pltpu.make_async_remote_copy(
        src_ref=src, dst_ref=dst, send_sem=send, recv_sem=recv, device_id=(dp, sp), device_id_type=MESH
    )


class Sends:
    def __init__(self, sems):
        self.sems = sems
        self.started = []

    def go(self, src, dst, recv, dp, sp, when=None):
        copy = remote(src, dst, self.sems.at[len(self.started)], recv, dp, sp)
        self.started.append((copy, when))
        if when is None:
            copy.start()
        else:
            pl.when(when)(copy.start)

    def finish(self):
        for copy, when in self.started:
            if when is None:
                copy.wait_send()
            else:
                pl.when(when)(copy.wait_send)


def arrived(dst, recv):
    dp, sp, _, _ = place()
    remote(dst, dst, recv, recv, dp, sp).wait_recv()


SCALE = 1.0 / math.sqrt(SIZE)
FACTOR = SCALE * math.log2(math.e)
ANY = pl.BlockSpec(memory_space=pl.ANY)
DMA = pltpu.SemaphoreType.DMA


def lanes_of(i, width):
    return pl.ds(pl.multiple_of(i * width, width), width)


def forward_heads(c, qs, band, lb, bias, pb, rb, aa, an, dp):
    cols = lanes_of(c, SIZE)
    for h in range(2):
        head = 2 * c + h
        lanes = lanes_of(head, SIZE)
        q = qs[:, lanes]
        scores = []
        top = None
        for b in range(KB):
            k = band[0, b // 2, pl.ds(b % 2 * SIZE, SIZE), cols]
            s = lax.dot_general(k, q, NT, preferred_element_type=F32)
            s = s + bias[b * SIZE : (b + 1) * SIZE, :] + lb[head, b : b + 1, :]
            scores.append(s)
            t = jnp.max(s, axis=0, keepdims=True)
            top = t if top is None else jnp.maximum(top, t)
        total = jnp.zeros((1, TOK), F32)
        for b in range(KB):
            p = jnp.exp2((scores[b] - top) * FACTOR)
            total = total + jnp.sum(p, axis=0, keepdims=True)
            pb[head, b * SIZE : (b + 1) * SIZE, :] = p.astype(BF)
        v = band[1, :, :, cols].reshape(BAND, SIZE)
        out = lax.dot_general(v, pb[head], TN, preferred_element_type=F32)
        inverse = 1.0 / total
        rb[head] = jnp.broadcast_to(inverse, (8, TOK))
        out = out * inverse
        aa[dp, lanes, :] = out.astype(BF)
        an[:, lanes] = out.T.astype(BF)


def backward_heads(c, qs, band, pb, rb, aa, gt, dp):
    cols = lanes_of(c, SIZE)
    k = band[0, :, :, cols].reshape(BAND, SIZE)
    v = band[1, :, :, cols].reshape(BAND, SIZE)
    dk = jnp.zeros((BAND, SIZE), F32)
    dv = jnp.zeros((BAND, SIZE), F32)
    for h in range(2):
        head = 2 * c + h
        lanes = lanes_of(head, SIZE)
        inverse = rb[head, 0:1, :]
        g_t = gt[lanes, :].astype(F32)
        delta = jnp.sum(g_t * aa[dp, lanes, :].astype(F32), axis=0, keepdims=True) * inverse
        g_t = g_t * inverse
        g = g_t.T.astype(BF)
        grad_p = jnp.dot(v, g_t.astype(BF), preferred_element_type=F32)
        p = pb[head]
        grad_s = (p.astype(F32) * (grad_p - delta)).astype(BF)
        dq_t = lax.dot_general(k, grad_s, TN, preferred_element_type=F32)
        dk = dk + jnp.dot(grad_s, qs[:, lanes], preferred_element_type=F32)
        dv = dv + jnp.dot(p, g, preferred_element_type=F32)
        qs[:, lanes] = (dq_t * SCALE).T.astype(BF)
    band[0, :, :, cols] = (dk * SCALE).astype(BF).reshape(5, TOK, SIZE)
    band[1, :, :, cols] = dv.astype(BF).reshape(5, TOK, SIZE)


def layer_kernel(
    q_ref, k_ref, v_ref, list_ref, cnt_ref, len_ref, w_ref, d_ref,
    lo_ref, dq_ref, gk_ref, gv_ref, gb_ref,
    band, raw, lb, wb, db, qs, ds, bias, pb, rb, aa, an, gt, back, gw, rs, rx, gsum,
    local, kv_send, kv_recv, w_send, w_recv, q_recv, pair_send, pair_recv, first_send, l_recv, d_recv,
    a_send, a_recv, row_send, row_recv, z_send, z_recv, rs_send, rs_recv, g_send, g_recv,
):
    dp, sp, z, x = place()
    y, core = dp // 2, dp % 2
    other = dp_at(y, 1 - core)
    loads = [
        pltpu.make_async_copy(k_ref, band.at[0, 4], local.at[0]),
        pltpu.make_async_copy(v_ref, band.at[1, 4], local.at[1]),
        pltpu.make_async_copy(w_ref.at[:, lanes_of(core, HALF)], wb.at[sp, :, lanes_of(core, HALF)], local.at[3]),
        pltpu.make_async_copy(d_ref.at[:, lanes_of(dp, PART)], db.at[dp], local.at[4]),
        pltpu.make_async_copy(q_ref, qs, local.at[5]),
        pltpu.make_async_copy(d_ref, ds, local.at[6]),
    ]
    for copy in loads:
        copy.start()
    greet()
    def chunks(row):
        return [(row + i) % 4 for i in (0, 1, 3, 2)]

    order = chunks(z)
    first_out = Sends(first_send)
    up, down = sp_at(z + 1, x), sp_at(z - 1, x)
    y_up, y_down, y_far = dp_at(y + 1, core), dp_at(y - 1, core), dp_at(y + 2, core)

    def kv_up(j):
        cols = lanes_of(j, 256)
        return remote(band.at[:, 4, :, cols], band.at[:, 0, :, cols], kv_send.at[0, j], kv_recv.at[0, j], dp, up)

    def kv_row(k, j):
        cols = lanes_of(j, 256)
        src = band.at[:, jnp.where(x + k < 4, 4, 0), :, cols]
        return remote(src, band.at[:, 4 - k, :, cols], kv_send.at[k, j], kv_recv.at[4 - k, j], dp, sp_at(z, x + k))

    def kv_rows(j, mine):
        for k in (2, 1, 3):
            pl.when((x + k < 4) if mine else (x + k >= 4))(kv_row(k, j).start)

    def kv_here(slot, j):
        arrived(band.at[:, slot, :, lanes_of(j, 256)], kv_recv.at[slot, j])

    half, other_half = lanes_of(core, HALF), lanes_of(1 - core, HALF)
    w_out = Sends(w_send)

    def weight(slot, first, rows, to):
        block = wb.at[slot, pl.ds(first, rows), half]
        w_out.go(block, block, w_recv.at[slot], dp, to)

    def weight_here(slot):
        arrived(wb.at[slot, :, half], w_recv.at[slot])

    def weight_quarter(slot, recv, to_dp, to_sp):
        block = wb.at[slot, pl.ds(pl.multiple_of(32 * y, 32), 32), half]
        w_out.go(block, block, recv, to_dp, to_sp)

    def weight_quarter_here(slot):
        arrived(wb.at[slot, pl.ds(0, 32), half], q_recv.at[slot])
        for dy in (1, 3, 2):
            weight_quarter(slot, w_recv.at[slot], dp_at(y + dy, core), sp)

    def weight_rest_here(slot):
        arrived(wb.at[slot, pl.ds(0, 96), half], w_recv.at[slot])

    def weight_z(slot):
        weight(slot, 0, 128, up)
        weight(slot, 0, 128, down)

    def weight_relay(dx, above):
        slot = sp_at(z + 1 if above else z - 1, x + dx)
        weight_here(slot)
        if above:
            weight(slot, 0, 96, down)
        else:
            weight(slot, 96, 32, up)

    def weight_pair(row):
        block = wb.at[pl.ds(4 * row, 4), :, half]
        remote(block, block, pair_send, pair_recv.at[row], other, sp).start()

    def grad_attn(row):
        arrived(wb.at[pl.ds(4 * row, 4), :, other_half], pair_recv.at[row])

        def one(i, _):
            i = 2 * row + i
            w = wb[pl.ds(2 * i, 2)].reshape(TOK, 3072)
            g = lax.dot_general(w, ds[...], NT, preferred_element_type=F32)
            gt[pl.ds(pl.multiple_of(i * TOK, TOK), TOK), :] = g.astype(BF)
            return 0

        lax.fori_loop(0, 2, one, 0)

    def spread(slot, j, first, rows, send, to):
        block = aa.at[slot, pl.ds(j * 512 + first, rows)]
        remote(block, block, send, a_recv.at[slot, j], to, sp).start()

    def spread_here(slot, j):
        arrived(aa.at[slot, pl.ds(j * 512, 512)], a_recv.at[slot, j])

    def spread_own(c):
        for i, to in enumerate((y_up, y_down, other)):
            spread(dp, c // 2, c % 2 * 256, 256, a_send.at[i], to)

    def spread_on(j):
        spread_here(y_down, j)
        spread(y_down, j, 0, 256, a_send.at[3], y_up)
        spread(y_down, j, 0, 512, a_send.at[4], other)
        spread_here(y_up, j)
        spread(y_up, j, 256, 256, a_send.at[5], y_down)
        spread(y_up, j, 0, 512, a_send.at[6], other)

    def spread_far(j):
        spread_here(y_far, j)
        spread(y_far, j, 0, 512, a_send.at[7], other)

    diagonal = lax.broadcasted_iota(jnp.int32, (32, 32), 0) == lax.broadcasted_iota(jnp.int32, (32, 32), 1)
    slot_of = lax.broadcasted_iota(jnp.int32, (32, 128), 1)
    listed = jnp.full((32, 128), -100, jnp.int32)
    for i in range(8):
        row = jnp.where(cnt_ref[...] > i, list_ref[i : i + 1, :], -100)
        listed = jnp.where(slot_of == i, jnp.max(jnp.where(diagonal, row, -100), axis=1, keepdims=True), listed)
    raw[sp] = listed

    for copy in loads[:3]:
        copy.wait()
    for dx in (1, 3, 2):
        weight_quarter(sp, q_recv.at[sp], dp, sp_at(z, x + dx))
    first, *others = chunks(z + 1)
    kv_up(first).start()
    kv_rows(order[0], True)
    weight_z(sp)
    for j in others:
        kv_up(j).start()
    for r in range(1, 16):
        first_out.go(raw.at[sp], raw.at[sp], l_recv, dp, (sp + r) % 16)

    q_pos = sp * TOK + lax.broadcasted_iota(jnp.int32, (1, TOK), 1)
    begin = jnp.zeros((1, TOK), jnp.int32)
    start = jnp.int32(0)
    for i in range(16):
        begin = jnp.where(q_pos >= start, start, begin)
        start = start + len_ref[0, i]

    def mask(b, _):
        rows = pl.ds(pl.multiple_of(b * SIZE, SIZE), SIZE)
        k_pos = (sp - HALO) * TOK + b * SIZE + lax.broadcasted_iota(jnp.int32, (SIZE, TOK), 0)
        bias[rows, :] = jnp.where((k_pos <= q_pos) & (k_pos >= begin), 0.0, NEG)
        return 0

    lax.fori_loop(0, KB, mask, 0)

    for dx in (1, 3, 2):
        weight_quarter_here(sp_at(z, x + dx))
    kv_rows(order[1], True)
    kv_here(0, order[0])
    kv_rows(order[0], False)
    for dx in (1, 3, 2):
        weight_rest_here(sp_at(z, x + dx))
        weight_z(sp_at(z, x + dx))
    weight_pair(z)
    for r in (2, 6, 4, 1, 3, 5, 7):
        to = (dp + r) % 8
        first_out.go(d_ref.at[:, lanes_of(to, PART)], db.at[dp], d_recv, to, sp)
    kv_here(0, order[1])
    kv_rows(order[1], False)
    kv_rows(order[2], True)
    arrived(raw.at[pl.ds(0, 15)], l_recv)

    def list_terms(h, _):
        ids = 2 * sp - 2 * HALO + lax.broadcasted_iota(jnp.int32, (16, 128), 0)
        for i in range(2):
            found = jnp.where(raw[h, pl.ds(2 * sp + i, 1), :] == ids, 0.0, NEG)
            found = jnp.max(found, axis=1, keepdims=True)
            lb[h, :, i * SIZE : (i + 1) * SIZE] = jnp.broadcast_to(found, (16, SIZE))
        return 0

    lax.fori_loop(0, 16, list_terms, 0)
    for copy in loads[3:]:
        copy.wait()
    kv_here(0, order[2])
    kv_rows(order[2], False)
    kv_rows(order[3], True)
    grad_attn(z)

    def forward(c, _):
        forward_heads(c, qs, band, lb, bias, pb, rb, aa, an, dp)
        spread_own(c)
        return 0

    def backward(c, _):
        backward_heads(c, qs, band, pb, rb, aa, gt, dp)
        cols = lanes_of(c, SIZE)
        for k in (2, 1, 3):
            remote(
                band.at[:, 4 - k, :, cols], back.at[k - 1, :, :, cols], row_send.at[k - 1], row_recv.at[k - 1, c], dp, sp_at(z, x - k)
            ).start()
        return 0

    def backward_chunk(j, between=None):
        cols = lanes_of(j, 256)
        for k in range(4):
            remote(band.at[:, 0, :, cols], band.at[:, 0, :, cols], kv_send.at[k, j], kv_send.at[k, j], dp, up).wait_send()
        if between is None:
            lax.fori_loop(2 * j, 2 * j + 2, backward, 0)
        else:
            lax.fori_loop(2 * j, 2 * j + 1, backward, 0)
            between()
            lax.fori_loop(2 * j + 1, 2 * j + 2, backward, 0)

    def spread_in(j):
        for r in range(4):
            spread_here(dp_at(y + r, 1 - core), j)

    def weight_grad(j):
        rows = pl.ds(pl.multiple_of(j * 512, 512), 512)
        total = jnp.zeros((512, PART), F32)
        for e in range(8):
            total = total + jnp.dot(aa[e, rows, :], db[e], preferred_element_type=F32)
        gw[pl.ds(4 * j, 4)] = total.astype(BF).reshape(4, 128, PART)

    def scatter_z(j):
        k = (z - j + 4) % 4 - 1
        remote(gw.at[pl.ds(4 * j, 4)], rs.at[pl.ds(4 * k, 4)], rs_send.at[0], rs_recv.at[0], dp, sp_at(j, x)).start()

    def kv_chunk(j):
        for slot in (3, 1, 2):
            kv_here(slot, j)

    def forward_chunk(j):
        lax.fori_loop(2 * j, 2 * j + 2, forward, 0)

    own_row, row_above, row_below, row_far = order

    def scatter(j):
        spread_in(j)
        weight_grad(j)
        if j is not own_row:
            scatter_z(j)

    kv_chunk(own_row)
    forward_chunk(own_row)
    kv_here(0, row_far)
    kv_rows(row_far, False)
    backward_chunk(own_row)
    weight_relay(0, True)
    weight_relay(0, False)

    kv_chunk(row_above)
    forward_chunk(row_above)
    for dx in (1, 3):
        weight_relay(dx, True)
        weight_relay(dx, False)
    spread_on(own_row)

    kv_chunk(row_below)
    forward_chunk(row_below)
    weight_relay(2, True)
    weight_pair(row_above)
    weight_relay(2, False)
    weight_pair(row_below)
    grad_attn(row_above)
    backward_chunk(row_above)
    spread_on(row_above)
    spread_far(own_row)
    grad_attn(row_below)
    backward_chunk(row_below)
    spread_on(row_below)
    spread_far(row_above)
    for i in range(4):
        weight_here(4 * row_far + i)
    weight_pair(row_far)

    kv_chunk(row_far)
    forward_chunk(row_far)
    arrived(db.at[pl.ds(0, 7)], d_recv)
    scatter(own_row)
    scatter(row_above)
    spread_far(row_below)
    grad_attn(row_far)
    scatter(row_below)
    backward_chunk(row_far, lambda: spread_on(row_far))
    dq_out = pltpu.make_async_copy(qs, dq_ref, local.at[7])
    dq_out.start()
    spread_far(row_far)
    scatter(row_far)

    keep = [jnp.where(x + k < 4, 1.0, 0.0).astype(F32) for k in (1, 2, 3)]

    def row_sums(j):
        def one(c, _):
            cols = lanes_of(c, SIZE)
            for k in range(3):
                arrived(back.at[k, :, :, cols], row_recv.at[k, c])
            below = band[:, 0, :, cols].astype(F32)
            here = band[:, 4, :, cols].astype(F32)
            for k in range(3):
                got = back[k, :, :, cols].astype(F32)
                here = here + got * keep[k]
                below = below + got * (1.0 - keep[k])
            band[:, 0, :, cols] = below.astype(BF)
            band[:, 4, :, cols] = here.astype(BF)
            remote(band.at[:, 0, :, cols], back.at[3, :, :, cols], z_send, z_recv.at[c], dp, down).start()
            return 0

        lax.fori_loop(2 * j, 2 * j + 2, one, 0)

    def project(i, _):
        cols = lanes_of(i, 512)
        w = wb[:, :, cols].reshape(2048, 512)
        ds[:, cols] = jnp.dot(an[...], w, preferred_element_type=F32).astype(BF)
        return 0

    lax.fori_loop(0, 6, project, 0)
    lo_out = pltpu.make_async_copy(ds, lo_ref, local.at[8])
    lo_out.start()

    row_sums(own_row)
    arrived(rs.at[pl.ds(0, 12)], rs_recv.at[0])

    def z_sums(i, _):
        total = gw[4 * z + i].astype(F32)
        for t in range(3):
            total = total + rs[4 * t + i].astype(F32)
        rs[12 + i] = total.astype(BF)

        @pl.when(i != x)
        def _():
            k = (x - i + 4) % 4 - 1
            remote(rs.at[12 + i], rx.at[k], rs_send.at[1], rs_recv.at[1], dp, sp_at(z, i)).start()

        return 0

    lax.fori_loop(0, 4, z_sums, 0)
    row_sums(row_above)
    row_sums(row_below)
    arrived(rx, rs_recv.at[1])
    total = rs[12 + x].astype(F32)
    for r in range(3):
        total = total + rx[r].astype(F32)
    gsum[...] = total.astype(BF)
    g_out = Sends(g_send)

    def g_block(e):
        return gb_ref.at[:, lanes_of(e, PART)]

    for to in (y_far, y_up, y_down, other):
        g_out.go(gsum, g_block(dp), g_recv.at[dp], to, sp)
    own_sum = pltpu.make_async_copy(gsum, gb_ref.at[:, lanes_of(dp, PART)], local.at[9])
    own_sum.start()

    row_sums(row_far)

    def last(c, _):
        cols = lanes_of(c, SIZE)
        arrived(back.at[3, :, :, cols], z_recv.at[c])
        band[:, 4, :, cols] = (band[:, 4, :, cols].astype(F32) + back[3, :, :, cols].astype(F32)).astype(BF)
        return 0

    for j in order:
        lax.fori_loop(2 * j, 2 * j + 2, last, 0)
    kv_outs = [
        pltpu.make_async_copy(band.at[0, 4], gk_ref, local.at[10]),
        pltpu.make_async_copy(band.at[1, 4], gv_ref, local.at[2]),
    ]
    for copy in kv_outs:
        copy.start()
    for slot in (y_up, y_down, y_far):
        arrived(g_block(slot), g_recv.at[slot])
        g_out.go(g_block(slot), g_block(slot), g_recv.at[slot], other, sp)
    for r in range(4):
        slot = dp_at(y + r, 1 - core)
        arrived(g_block(slot), g_recv.at[slot])
    first_out.finish()
    w_out.finish()
    some = wb.at[:, :, half]
    remote(some, some, pair_send, pair_send, other, sp).wait_send()
    for i in range(8):
        some = aa.at[dp, pl.ds(0, 1024 if i in (3, 5) else 2048)]
        remote(some, some, a_send.at[i], a_send.at[i], other, sp).wait_send()
    for k in range(3):
        remote(back.at[k], back.at[k], row_send.at[k], row_send.at[k], dp, up).wait_send()
    remote(band.at[:, 0], band.at[:, 0], z_send, z_send, dp, down).wait_send()
    remote(rs.at[pl.ds(0, 12)], rs.at[pl.ds(0, 12)], rs_send.at[0], rs_send.at[0], dp, up).wait_send()
    remote(rx, rx, rs_send.at[1], rs_send.at[1], dp, up).wait_send()
    g_out.finish()
    for copy in (dq_out, lo_out, own_sum, *kv_outs):
        copy.wait()


def call_layer(q, k, v, lists, counts, lengths, w, d):
    vmem = pltpu.VMEM
    return pl.pallas_call(
        layer_kernel,
        in_specs=[ANY] * 3
        + [pl.BlockSpec(memory_space=vmem)] * 2
        + [pl.BlockSpec(memory_space=pltpu.SMEM)]
        + [ANY] * 2,
        out_specs=[ANY] * 5,
        out_shape=[
            jax.ShapeDtypeStruct((TOK, 3072), BF),
            jax.ShapeDtypeStruct((TOK, 2048), BF),
            jax.ShapeDtypeStruct((TOK, 1024), BF),
            jax.ShapeDtypeStruct((TOK, 1024), BF),
            jax.ShapeDtypeStruct((128, 3072), BF),
        ],
        scratch_shapes=[
            vmem((2, 5, TOK, 1024), BF),
            vmem((16, 32, 128), jnp.int32),
            vmem((16, 16, TOK), F32),
            vmem((16, 128, 3072), BF),
            vmem((8, TOK, PART), BF),
            vmem((TOK, 2048), BF),
            vmem((TOK, 3072), BF),
            vmem((BAND, TOK), F32),
            vmem((16, BAND, TOK), BF),
            vmem((16, 8, TOK), F32),
            vmem((8, 2048, TOK), BF),
            vmem((TOK, 2048), BF),
            vmem((2048, TOK), BF),
            vmem((4, 2, TOK, 1024), BF),
            vmem((16, 128, PART), BF),
            vmem((16, 128, PART), BF),
            vmem((3, 128, PART), BF),
            vmem((128, PART), BF),
            DMA((11,)),
            DMA((4, 4)),
            DMA((4, 4)),
            DMA((28,)),
            DMA((16,)),
            DMA((16,)),
            DMA,
            DMA((4,)),
            DMA((22,)),
            DMA,
            DMA,
            DMA((8,)),
            DMA((8, 4)),
            DMA((3,)),
            DMA((3, 8)),
            DMA,
            DMA((8,)),
            DMA((2,)),
            DMA((2,)),
            DMA((7,)),
            DMA((8,)),
        ],
        compiler_params=pltpu.CompilerParams(collective_id=0, has_side_effects=True, vmem_limit_bytes=60 * 2**20),
        cost_estimate=pl.CostEstimate(flops=27 * 10**9, bytes_accessed=20 * 10**6, transcendentals=6 * 10**6),
    )(q, k, v, lists, counts, lengths, w, d)


def per_device(queries, keys, values, key_blocks, block_counts, doc_lengths, out_weight, d_out):
    layer_out, grad_q, grad_k, grad_v, grad_all = call_layer(
        queries[0], keys[0], values[0], key_blocks[0, 0].T, block_counts[0], doc_lengths, out_weight, d_out[0]
    )
    grad_weight = grad_all.astype(F32)
    tokens = lax.axis_size("dp") * lax.axis_size("sp") * TOK
    grad_weight = grad_weight * (1.0 / math.sqrt(tokens))
    return (layer_out[None], grad_q[None], grad_k[None], grad_v[None], grad_weight)


def solution(mesh):
    in_specs = (
        P("dp", "sp", None),
        P("dp", "sp", None),
        P("dp", "sp", None),
        P("dp", "sp", None, None),
        P("dp", "sp", None),
        P("dp", None),
        P("sp", None),
        P("dp", "sp", None),
    )
    out_specs = (
        P("dp", "sp", None),
        P("dp", "sp", None),
        P("dp", "sp", None),
        P("dp", "sp", None),
        P("sp", None),
    )
    return jax.shard_map(per_device, mesh=mesh, in_specs=in_specs, out_specs=out_specs, check_vma=False)
```
